256 devices in a mesh: branch: 2 (over core), head: 8 (over z), seq: 16 (over y, x).
Axes of the slice: x: 4, y: 4, z: 8, core: 2. Of those that a mesh axis runs over, the one named last changes fastest.
Arguments:
- hidden: bfloat16 [2, 16384, 3072], P('branch', 'seq', 'head'), may hold values from -4.1875 to 4.1875
- modulation: float32 [2, 3, 3072], P('branch'), may hold values from 0.3 to 1.5
- branch_cache: bfloat16 [2, 16384, 3072], P('branch', 'seq', 'head'), may hold values from -4.78125 to 4.78125
- k_cache: bfloat16 [2, 16384, 2048], P('branch', 'seq', 'head'), may hold values from -136 to 136
- v_cache: bfloat16 [2, 16384, 2048], P('branch', 'seq', 'head'), may hold values from -6 to 6
- w_qkv: bfloat16 [3072, 3, 2048], P('branch', None, 'head'), may hold values from -0.109375 to 0.109375
- w_mlp_in: bfloat16 [3072, 6144], P('branch', 'head'), may hold values from -0.109375 to 0.109375
- w_attn_out: bfloat16 [2048, 3072], P('head', 'branch'), may hold values from -0.125 to 0.125
- w_mlp_out: bfloat16 [6144, 3072], P('head', 'branch'), may hold values from -0.078125 to 0.078125
- q_gain: float32 [128], replicated, may hold values from 1 to 3
- k_gain: float32 [128], replicated, may hold values from 1 to 3
- blocks: int32 [16, 2], P('seq'), may hold values from 0 to 7, as said below
- counts: int32 [16], P('seq'), may hold values from 1 to 2, as said below
Outputs:
- guided: bfloat16 [16384, 3072], P('seq', 'head')
The draws below stay inside these ranges and needn't reach their ends.
Inputs may be any that keep to these rules, and one draw needn't show every extreme that they name: `blocks`: each row holds 2 different block numbers; only the first counts[r] of row r are live. `counts`: some index of seq has 2 live blocks and some has 1.
All inputs are finite; a program needn't handle non-finite values.
Results may differ from the reference program's by a relative error of at most 0.015.
The reference program's roundings to bfloat16 on the way (of `picked`, `modulated`, `activation`, `attended`, `branch_new` and `branch_all`) count: a program that leaves them out, or rounds other values in their place, can miss the bound.
Values may be sent and summed in bfloat16 or wider, within the bound.
No kernel may reach another device: no remote copies, remote signals or barrier semaphores. Data moves between devices by JAX's collectives and lax.ppermute only.
A program may use at most 192 MiB of HBM per device.

```python
import math
import jax
import jax.numpy as jnp
from jax import lax

D = 3072
HEADS = 16
HDIM = 128
FF = 6144
BLOCK = 128
ROWS_DEV = 1024
MAXB = 2
S = 16384
HD = 2048
N_BRANCH = 2
N_SEQ = 16


def draw_blocks(key, part):
    key = jax.random.fold_in(key, 11)
    key_list = jax.random.split(key, N_SEQ)
    orders = jax.vmap(lambda one_key: jax.random.permutation(one_key, ROWS_DEV // BLOCK))(key_list)
    return orders[:, :MAXB].astype(jnp.int32)


def draw_counts(key, part):
    key = jax.random.fold_in(key, 23)
    first_key, second_key, third_key = jax.random.split(key, 3)
    lowest = max(1, ROWS_DEV // BLOCK // 10)
    result = jax.random.randint(first_key, (N_SEQ,), lowest, MAXB + 1).astype(jnp.int32)
    chosen = jax.random.randint(second_key, (), 0, N_SEQ)
    offset = jax.random.randint(third_key, (), 0, N_SEQ - 1)
    result = result.at[chosen].set(MAXB)
    result = result.at[(chosen + 1 + offset) % N_SEQ].set(lowest)
    return result.astype(jnp.int32)


def draw_k_cache(key, part):
    key = jax.random.fold_in(key, 37)
    first_key = jax.random.fold_in(key, 0)
    shape = (N_BRANCH, S, HD)
    base = jax.random.normal(first_key, shape, jnp.float32) * 2.0
    return jnp.clip(base, -12.0, 12.0).astype(jnp.bfloat16)


def block_scale(rng, shape, pieces, smallest, largest):
    level = 1.0
    for position, blocks in pieces:
        heights = jax.random.uniform(jax.random.fold_in(jax.random.fold_in(rng, 6), position), (blocks,), jnp.float32, smallest / len(pieces), largest / len(pieces))
        level = level * jnp.repeat(jnp.exp(heights), shape[position] // blocks).reshape((-1,) + (1,) * (len(shape) - 1 - position))
    return level


def scatter_about(key, dims, spread, bound, shards=(), held_as=jnp.bfloat16):
    values = jax.random.normal(key, dims, jnp.float32) * spread
    if len(shards) > 0:
        values = block_scale(key, dims, shards, -0.22, 0.18) * values
    return jnp.clip(values, min=-bound, max=bound).astype(held_as)


def setup_inputs(seed: int = 0) -> dict:
    splits = jax.random.split(jax.random.key(seed), 14)
    return {
        "hidden": scatter_about(splits[0], (N_BRANCH, S, D), 0.7, 4.1875, ((0, 2), (1, 16), (2, 8))),
        "modulation": jnp.clip(0.3 + 1.2 * jax.random.uniform(splits[1], (N_BRANCH, 3, D), jnp.float32) ** block_scale(splits[1], (N_BRANCH, 3, D), ((0, 2),), -0.2, 0.2), 0.3, 1.5),
        "branch_cache": scatter_about(splits[2], (N_BRANCH, S, D), 0.8, 4.78125, ((0, 2), (1, 16), (2, 8))),
        "k_cache": draw_k_cache(jax.random.fold_in(splits[13], 71), 0),
        "v_cache": scatter_about(splits[4], (N_BRANCH, S, HD), 1.0, 6.0, ((0, 2), (1, 16), (2, 8))),
        "w_qkv": scatter_about(splits[5], (D, 3, HD), D ** -0.5, 0.109375, ((0, 2), (2, 8))),
        "w_mlp_in": scatter_about(splits[6], (D, FF), D ** -0.5, 0.109375, ((0, 2), (1, 8))),
        "w_attn_out": scatter_about(splits[7], (HD, D), HD ** -0.5, 0.125, ((0, 8), (1, 2))),
        "w_mlp_out": scatter_about(splits[8], (FF, D), FF ** -0.5, 0.078125, ((0, 8), (1, 2))),
        "q_gain": jnp.clip(jnp.exp(jax.random.uniform(splits[9], (HDIM,), jnp.float32, math.log(1.0), math.log(3.0))), 1.0, 3.0),
        "k_gain": jnp.clip(jnp.exp(jax.random.uniform(splits[10], (HDIM,), jnp.float32, math.log(1.0), math.log(3.0))), 1.0, 3.0),
        "blocks": draw_blocks(jax.random.fold_in(splits[13], 71), 0),
        "counts": draw_counts(jax.random.fold_in(splits[13], 71), 0),
    }


GUIDANCE = 1.5
EPSILON = 1e-06

def layer_norm(picked, shift_row, scale_row):
    values = picked.astype(jnp.float32)
    centred = values - lax.optimization_barrier(jnp.mean(values, axis=-1, keepdims=True))
    variance = lax.optimization_barrier(jnp.mean(centred * centred, axis=-1, keepdims=True))
    return (centred * lax.rsqrt(variance + EPSILON) * (1.0 + scale_row) + shift_row).astype(jnp.bfloat16)

def head_norm(values, gain, head_count):
    shaped = values.reshape(values.shape[0], head_count, -1)
    power = lax.optimization_barrier(jnp.mean(shaped * shaped, axis=-1, keepdims=True))
    return (shaped * lax.rsqrt(power + EPSILON) * gain).astype(jnp.bfloat16)

def reference(hidden, modulation, branch_cache, k_cache, v_cache, w_qkv, w_mlp_in, w_attn_out, w_mlp_out, q_gain, k_gain, blocks, counts):
    block_count = ROWS_DEV // BLOCK
    slot_ids = jnp.arange(MAXB, dtype=jnp.int32)
    slot_match = (blocks[:, :, None] == jnp.arange(block_count, dtype=jnp.int32)[None, None, :]) & (slot_ids[None, :, None] < counts[:, None, None])
    renewed = jnp.any(slot_match, axis=1)
    slot_of = lax.optimization_barrier(jnp.sum(jnp.where(slot_match, slot_ids[None, :, None], 0), axis=1)).astype(jnp.int32)
    anchor = (jnp.arange(N_SEQ, dtype=jnp.int32)[:, None] * block_count + blocks).reshape(-1).astype(jnp.int32)
    flat_qkv = w_qkv.reshape(D, 3 * HD)

    def renew(cached, fresh):
        width_here = cached.shape[-1]
        stale = cached.reshape(N_SEQ, block_count, BLOCK, width_here)
        placed = fresh.reshape(N_SEQ, MAXB, BLOCK, width_here)
        placed = jax.vmap(lambda group, index: group[index])(placed, slot_of)
        return jnp.where(renewed[:, :, None, None], placed, stale).reshape(S, width_here)

    def one_head(triple):
        query_head, key_head, value_head = triple
        scores = jnp.dot(query_head, key_head.T, preferred_element_type=jnp.float32) * HDIM ** (-0.5)
        top_score = lax.optimization_barrier(jnp.max(scores, axis=1, keepdims=True))
        weights = jnp.exp(scores - top_score)
        total = lax.optimization_barrier(jnp.sum(weights, axis=1, keepdims=True))
        return jnp.dot(weights.astype(jnp.bfloat16), value_head, preferred_element_type=jnp.float32) / total

    def one_branch(branch_id):
        tokens = hidden[branch_id]
        picked = tokens.reshape(N_SEQ * block_count, BLOCK, D)[anchor].reshape(-1, D)
        modulated = layer_norm(picked, modulation[branch_id, 0], modulation[branch_id, 1])
        qkv = jnp.dot(modulated, flat_qkv, preferred_element_type=jnp.float32)
        mlp_pre = jnp.dot(modulated, w_mlp_in, preferred_element_type=jnp.float32)
        queries = head_norm(qkv[:, :HD], q_gain, HEADS)
        keys_new = head_norm(qkv[:, HD:2 * HD], k_gain, HEADS).reshape(-1, HD)
        values_new = qkv[:, 2 * HD:].astype(jnp.bfloat16)
        activation = jax.nn.gelu(mlp_pre, approximate=True).astype(jnp.bfloat16)
        keys_all = renew(k_cache[branch_id], keys_new).reshape(S, HEADS, HDIM)
        values_all = renew(v_cache[branch_id], values_new).reshape(S, HEADS, HDIM)
        attended = lax.map(one_head, (jnp.transpose(queries, (1, 0, 2)), jnp.transpose(keys_all, (1, 0, 2)), jnp.transpose(values_all, (1, 0, 2))))
        attended = jnp.transpose(attended, (1, 0, 2)).reshape(-1, HD).astype(jnp.bfloat16)
        branch_new = (jnp.dot(attended, w_attn_out, preferred_element_type=jnp.float32) + jnp.dot(activation, w_mlp_out, preferred_element_type=jnp.float32)).astype(jnp.bfloat16)
        branch_all = renew(branch_cache[branch_id], branch_new)
        return tokens.astype(jnp.float32) + modulation[branch_id, 2] * branch_all.astype(jnp.float32)
    return ((1.0 - GUIDANCE) * one_branch(0) + GUIDANCE * one_branch(1)).astype(jnp.bfloat16)
```

```python
import functools

import jax
import jax.numpy as jnp
from jax import lax
from jax.experimental import pallas as pl
from jax.experimental.pallas import tpu as pltpu
from jax.sharding import PartitionSpec as P

HDIM = 128
BLOCK = 128
GUIDANCE = 1.5
EPSILON = 1e-06
LOG2E = 1.4426950408889634
HEAD = 8
SIDE = 4
STALE = 6
STAT_ROWS = 16
VMEM_LIMIT = 48 * 1024 * 1024

F32 = jnp.float32
BF16 = jnp.bfloat16


def whole():
    return pl.BlockSpec(memory_space=pltpu.VMEM)


def scalars():
    return pl.BlockSpec(memory_space=pltpu.SMEM)


def params():
    return pltpu.CompilerParams(vmem_limit_bytes=VMEM_LIMIT)


def dot(left, right):
    return jnp.dot(left, right, preferred_element_type=F32)


def pick_kernel(blocks_ref, first_ref, second_ref, out_first, out_second):
    out_first[...] = first_ref[...]
    out_second[...] = second_ref[...]


def pick(tokens, blocks):
    width = tokens.shape[1]
    shape = jax.ShapeDtypeStruct((BLOCK, width), BF16)
    return pl.pallas_call(
        pick_kernel,
        grid_spec=pltpu.PrefetchScalarGridSpec(
            num_scalar_prefetch=1,
            grid=(1,),
            in_specs=[
                pl.BlockSpec((BLOCK, width), lambda i, s: (s[0, 0], 0)),
                pl.BlockSpec((BLOCK, width), lambda i, s: (s[0, 1], 0)),
            ],
            out_specs=[pl.BlockSpec((BLOCK, width), lambda i, s: (0, 0))] * 2,
        ),
        out_shape=[shape, shape],
        compiler_params=params(),
        name="pick_rows",
    )(blocks, tokens, tokens)


def stale_index(i, s):
    low = jnp.minimum(s[0, 0], s[0, 1])
    high = jnp.maximum(s[0, 0], s[0, 1])
    index = i + (i >= low).astype(jnp.int32)
    return index + (index >= high).astype(jnp.int32)


def pack_kernel(blocks_ref, k_ref, v_ref, first_ref, second_ref):
    first_ref[:, :HDIM] = k_ref[:, :HDIM]
    first_ref[:, HDIM:] = v_ref[:, :HDIM]
    second_ref[:, :HDIM] = k_ref[:, HDIM:]
    second_ref[:, HDIM:] = v_ref[:, HDIM:]


def pack_stale(keys, values, blocks):
    block = (BLOCK, 2 * HDIM)
    shape = jax.ShapeDtypeStruct((STALE * BLOCK, 2 * HDIM), BF16)
    return pl.pallas_call(
        pack_kernel,
        grid_spec=pltpu.PrefetchScalarGridSpec(
            num_scalar_prefetch=1,
            grid=(STALE,),
            in_specs=[pl.BlockSpec(block, lambda i, s: (stale_index(i, s), 0))] * 2,
            out_specs=[pl.BlockSpec(block, lambda i, s: (i, 0))] * 2,
        ),
        out_shape=[shape, shape],
        compiler_params=params(),
        name="pack_stale",
    )(blocks, keys, values)


def project_kernel(blocks_ref, counts_ref, where_ref, *refs):
    chunks = refs[:16]
    mod_ref, own_ref, other_ref, q_gain_ref, k_gain_ref, k_old_ref, v_old_ref = refs[16:23]
    x_ref, y_ref, rows_ref = refs[23:]
    core = where_ref[0]
    z = where_ref[1]
    width = chunks[0].shape[1]
    full = HEAD * width
    step = 32
    for slot in range(2):
        group = chunks[slot * HEAD : (slot + 1) * HEAD]
        for row in range(0, BLOCK, step):
            values = [ref[row : row + step, :].astype(F32) for ref in group]
            mean = sum(jnp.sum(v, axis=-1, keepdims=True) for v in values) / full
            centred = [v - mean for v in values]
            var = sum(jnp.sum(c * c, axis=-1, keepdims=True) for c in centred) / full
            inverse = lax.rsqrt(var + EPSILON)
            for k in range(HEAD):
                owner = lax.rem(z - k + HEAD, HEAD)
                columns = pl.ds(pl.multiple_of(owner * width, width), width)
                shift = mod_ref[0:1, columns]
                scale = mod_ref[1:2, columns]
                rows_ref[slot * BLOCK + row : slot * BLOCK + row + step, columns] = (
                    centred[k] * inverse * (1.0 + scale) + shift
                ).astype(BF16)
    half = full // 2
    here = pl.ds(pl.multiple_of(core * half, half), half)
    there = pl.ds(pl.multiple_of((1 - core) * half, half), half)
    total = dot(rows_ref[:, here], own_ref[...]) + dot(rows_ref[:, there], other_ref[...])

    def norm(values, gain_ref):
        power = jnp.mean(values * values, axis=-1, keepdims=True)
        return (values * lax.rsqrt(power + EPSILON) * gain_ref[...]).astype(BF16)

    live = counts_ref[0] > 1
    for head, fresh_ref, query_ref in ((0, x_ref, y_ref), (1, y_ref, x_ref)):
        at = head * HDIM
        query_ref[:, 2 * HDIM :] = norm(total[:, at : at + HDIM], q_gain_ref)
        key = norm(total[:, 2 * HDIM + at : 3 * HDIM + at], k_gain_ref)
        value = total[:, 4 * HDIM + at : 5 * HDIM + at].astype(BF16)
        fresh_ref[:BLOCK, :HDIM] = key[:BLOCK]
        fresh_ref[:BLOCK, HDIM : 2 * HDIM] = value[:BLOCK]
        fresh_ref[BLOCK:, :HDIM] = jnp.where(live, key[BLOCK:], k_old_ref[:, at : at + HDIM])
        fresh_ref[BLOCK:, HDIM : 2 * HDIM] = jnp.where(
            live, value[BLOCK:], v_old_ref[:, at : at + HDIM]
        )


def project(blocks, counts, where, chunks, modulation, own, other, q_gain, k_gain, keys, values):
    full = HEAD * chunks[0].shape[1]
    rows = 2 * BLOCK
    whole_block = lambda a: pl.BlockSpec(a.shape, lambda i, *s: (0,) * a.ndim)
    old = pl.BlockSpec((BLOCK, 2 * HDIM), lambda i, blocks, counts, where: (blocks[0, 1], 0))
    plain = [*chunks, modulation, own, other, q_gain, k_gain]
    outs = [
        jax.ShapeDtypeStruct((rows, 3 * HDIM), BF16),
        jax.ShapeDtypeStruct((rows, 3 * HDIM), BF16),
        jax.ShapeDtypeStruct((rows, full), BF16),
    ]
    return pl.pallas_call(
        project_kernel,
        grid_spec=pltpu.PrefetchScalarGridSpec(
            num_scalar_prefetch=3,
            grid=(1,),
            in_specs=[whole_block(a) for a in plain] + [old, old],
            out_specs=[whole_block(a) for a in outs],
        ),
        out_shape=outs,
        compiler_params=params(),
        cost_estimate=pl.CostEstimate(
            flops=2 * rows * full * 6 * HDIM, bytes_accessed=8 * 2**20, transcendentals=0
        ),
        name="project",
    )(blocks, counts, where, *plain, keys, values)


def hidden_kernel(where_ref, rows_ref, own_ref, other_ref, mine_ref, theirs_ref):
    core = where_ref[0]
    half = own_ref.shape[0]
    here = pl.ds(pl.multiple_of(core * half, half), half)
    there = pl.ds(pl.multiple_of((1 - core) * half, half), half)
    total = dot(rows_ref[:, here], own_ref[...]) + dot(rows_ref[:, there], other_ref[...])
    active = jax.nn.gelu(total, approximate=True).astype(BF16)
    first = core == 0
    mine_ref[...] = jnp.where(first, active[:BLOCK], active[BLOCK:])
    theirs_ref[...] = jnp.where(first, active[BLOCK:], active[:BLOCK])


def hidden_units(where, rows, own, other):
    units = own.shape[1]
    shape = jax.ShapeDtypeStruct((BLOCK, units), BF16)
    return pl.pallas_call(
        hidden_kernel,
        in_specs=[scalars()] + [whole()] * 3,
        out_specs=[whole()] * 2,
        out_shape=[shape, shape],
        compiler_params=params(),
        cost_estimate=pl.CostEstimate(
            flops=2 * rows.shape[0] * rows.shape[1] * units,
            bytes_accessed=8 * 2**20,
            transcendentals=rows.shape[0] * units,
        ),
        name="hidden_units",
    )(where, rows, own, other)


def gated(core, left_own, left_other, w_own, w_other, gate_own, gate_other, emit):
    width = w_own.shape[1] // (HEAD // 2)
    for weights, side in ((w_own, core), (w_other, 1 - core)):
        for i in range(HEAD // 2):
            part = weights[:, i * width : (i + 1) * width]
            chunk = side * (HEAD // 2) + i
            value = dot(left_own, part) * gate_own[chunk] + dot(left_other, part) * gate_other[chunk]
            emit(chunk, value)


def units_out_kernel(
    where_ref, mine_ref, theirs_ref, own_ref, other_ref, gate_ref, gate_other_ref, out_ref
):
    def emit(chunk, value):
        out_ref[chunk] = value

    gated(
        where_ref[0], mine_ref[...], theirs_ref[...], own_ref, other_ref, gate_ref,
        gate_other_ref, emit,
    )


def heads_out_kernel(
    where_ref, mine_ref, theirs_ref, own_ref, other_ref, gate_ref, gate_other_ref, base_ref, out_ref
):
    def emit(chunk, value):
        out_ref[chunk] = (base_ref[chunk] + value).astype(BF16)

    gated(
        where_ref[0], mine_ref[...], theirs_ref[...], own_ref, other_ref, gate_ref,
        gate_other_ref, emit,
    )


def out_product(kernel, dtype, name, where, mine, theirs, own, other, gate, gate_other, *base):
    width = own.shape[1] // (HEAD // 2)
    return pl.pallas_call(
        kernel,
        in_specs=[scalars()] + [whole()] * (6 + len(base)),
        out_specs=whole(),
        out_shape=jax.ShapeDtypeStruct((HEAD, BLOCK, width), dtype),
        compiler_params=params(),
        cost_estimate=pl.CostEstimate(
            flops=8 * BLOCK * own.shape[0] * own.shape[1],
            bytes_accessed=6 * 2**20,
            transcendentals=0,
        ),
        name=name,
    )(where, mine, theirs, own, other, gate, gate_other, *base)


def attend_kernel(*refs):
    stale_x, stale_y = refs[0:4], refs[4:8]
    fresh_x, fresh_y = refs[8:12], refs[12:16]
    outs = refs[16:24]
    key_s, query_s, score_s, result_s, stat_s = refs[24:]
    piece = (STALE + 2) * BLOCK
    rows = 2 * BLOCK
    unit = LOG2E * HDIM**-0.5
    for head, (stale, fresh, asked) in enumerate(
        ((stale_x, fresh_x, fresh_y), (stale_y, fresh_y, fresh_x))
    ):
        for k in range(SIDE):
            key_s[head, k * piece : k * piece + STALE * BLOCK, :] = stale[k][...]
            key_s[head, k * piece + STALE * BLOCK : (k + 1) * piece, :] = fresh[k][:, : 2 * HDIM]
            query_s[head * SIDE + k] = asked[k][:, 2 * HDIM :]
    stat_s[...] = jnp.zeros_like(stat_s)

    def tile(index, carry):
        head = index // SIDE
        query = query_s[index]
        top = None
        for k in range(SIDE):
            keys = key_s[head, k * piece : (k + 1) * piece, :HDIM]
            scores = lax.dot_general(
                query, keys, (((1,), (1,)), ((), ())), preferred_element_type=F32
            )
            score_s[:, k * piece : (k + 1) * piece] = scores
            here = jnp.max(scores, axis=-1, keepdims=True)
            top = here if top is None else jnp.maximum(top, here)
        top = top * unit
        total = jnp.zeros((rows, 1), F32)
        summed = jnp.zeros((rows, HDIM), F32)
        for k in range(SIDE):
            weights = jnp.exp2(score_s[:, k * piece : (k + 1) * piece] * unit - top)
            total = total + jnp.sum(weights, axis=-1, keepdims=True)
            summed = summed + dot(
                weights.astype(BF16), key_s[head, k * piece : (k + 1) * piece, HDIM:]
            )
        result_s[index] = (summed / total).astype(BF16)
        lane = lax.broadcasted_iota(jnp.int32, (rows, HDIM), 1)
        stat_s[...] = jnp.where(lane == index, top + jnp.log2(total), stat_s[...])
        return carry

    lax.fori_loop(0, 2 * SIDE, tile, 0)
    stats = jnp.transpose(stat_s[...])
    for index in range(2 * SIDE):
        outs[index][:rows, :] = result_s[index]
        row = stats[index : index + 1, :]
        high = row.astype(BF16).astype(F32)
        middle = (row - high).astype(BF16).astype(F32)
        low = row - high - middle
        parts = [p[:, at : at + HDIM] for p in (high, middle, low) for at in (0, HDIM)]
        parts.append(jnp.zeros((STAT_ROWS - 6, HDIM), F32))
        outs[index][rows:, :] = jnp.concatenate(parts, axis=0).astype(BF16)


def attend(stale_x, stale_y, fresh_x, fresh_y):
    rows = 2 * BLOCK
    keys = SIDE * (STALE + 2) * BLOCK
    shape = jax.ShapeDtypeStruct((rows + STAT_ROWS, HDIM), BF16)
    outs = pl.pallas_call(
        attend_kernel,
        in_specs=[whole()] * 16,
        out_specs=[whole()] * 8,
        out_shape=[shape] * 8,
        scratch_shapes=[
            pltpu.VMEM((2, keys, 2 * HDIM), BF16),
            pltpu.VMEM((2 * SIDE, rows, HDIM), BF16),
            pltpu.VMEM((rows, keys), F32),
            pltpu.VMEM((2 * SIDE, rows, HDIM), BF16),
            pltpu.VMEM((rows, HDIM), F32),
        ],
        compiler_params=params(),
        cost_estimate=pl.CostEstimate(
            flops=4 * 2 * SIDE * rows * keys * HDIM,
            bytes_accessed=8 * 2**20,
            transcendentals=2 * SIDE * rows * keys,
        ),
        name="attend",
    )(*stale_x, *stale_y, *fresh_x, *fresh_y)
    return outs[:SIDE], outs[SIDE:]


def join_kernel(where_ref, *refs):
    parts, (mine_ref, theirs_ref) = refs[:8], refs[8:]
    rows = 2 * BLOCK
    stats = []
    for part in parts:
        tail = part[rows:, :].astype(F32)
        joined = [jnp.concatenate([tail[i : i + 1], tail[i + 1 : i + 2]], axis=1) for i in (0, 2, 4)]
        stats.append(joined[0] + joined[1] + joined[2])
    stats = jnp.concatenate(stats + [jnp.zeros((HDIM - 2 * SIDE, rows), F32)], axis=0)
    columns = jnp.transpose(stats)
    first = where_ref[0] == 0
    for head in range(2):
        level = [columns[:, head * SIDE + k : head * SIDE + k + 1] for k in range(SIDE)]
        top = functools.reduce(jnp.maximum, level)
        shares = [jnp.exp2(value - top) for value in level]
        inverse = 1.0 / sum(shares)
        result = sum(
            (shares[k] * inverse) * parts[head * SIDE + k][:rows, :].astype(F32)
            for k in range(SIDE)
        ).astype(BF16)
        at = slice(head * HDIM, (head + 1) * HDIM)
        mine_ref[:, at] = jnp.where(first, result[:BLOCK], result[BLOCK:])
        theirs_ref[:, at] = jnp.where(first, result[BLOCK:], result[:BLOCK])


def join(where, parts):
    shape = jax.ShapeDtypeStruct((BLOCK, 2 * HDIM), BF16)
    return pl.pallas_call(
        join_kernel,
        in_specs=[scalars()] + [whole()] * 8,
        out_specs=[whole()] * 2,
        out_shape=[shape, shape],
        compiler_params=params(),
        name="join",
    )(where, *parts)


def finish_kernel(where_ref, parts_ref, own_ref, other_ref, stale_ref, out_ref):
    factor = jnp.where(where_ref[0] == 0, 1.0 - GUIDANCE, GUIDANCE)
    total = parts_ref[0].astype(F32)
    for k in range(1, HEAD):
        total = total + parts_ref[k].astype(F32)
    total = total + factor * own_ref[...].astype(F32) + (1.0 - factor) * other_ref[...].astype(F32)
    out_ref[...] = jnp.where(where_ref[2] > 0, total.astype(BF16), stale_ref[...])


def finish(where, parts, own, other, stale):
    width = own.shape[1]
    block = pl.BlockSpec((BLOCK, width), lambda i, where: (where[3], 0))
    return pl.pallas_call(
        finish_kernel,
        grid_spec=pltpu.PrefetchScalarGridSpec(
            num_scalar_prefetch=1,
            grid=(1,),
            in_specs=[
                pl.BlockSpec((HEAD, BLOCK, width), lambda i, where: (0, 0, 0)),
                block,
                block,
                block,
            ],
            out_specs=pl.BlockSpec((BLOCK, width), lambda i, where: (0, 0)),
        ),
        out_shape=jax.ShapeDtypeStruct((BLOCK, width), BF16),
        compiler_params=params(),
        name="finish",
    )(where, parts, own, other, stale)


def ring(array, shift):
    return lax.ppermute(array, "head", [(i, (i + shift) % HEAD) for i in range(HEAD)])


def swap(array):
    return lax.ppermute(array, "branch", [(0, 1), (1, 0)])


def along_x(array, shift):
    pairs = [
        (y * SIDE + x, y * SIDE + (x + shift) % SIDE) for y in range(SIDE) for x in range(SIDE)
    ]
    return lax.ppermute(array, "seq", pairs)


def along_y(array, shift):
    pairs = [
        (y * SIDE + x, (y + shift) % SIDE * SIDE + x) for y in range(SIDE) for x in range(SIDE)
    ]
    return lax.ppermute(array, "seq", pairs)


def local(
    hidden,
    modulation,
    branch_cache,
    k_cache,
    v_cache,
    w_qkv,
    w_mlp_in,
    w_attn_out,
    w_mlp_out,
    q_gain,
    k_gain,
    blocks,
    counts,
):
    core = lax.axis_index("branch")
    z = lax.axis_index("head")
    own_slot = jnp.where(core == 0, blocks[0, 0], blocks[0, 1])
    other_slot = jnp.where(core == 0, blocks[0, 1], blocks[0, 0])
    where = jnp.stack([core, z, (core < counts[0]).astype(jnp.int32), own_slot])
    tokens, cached = hidden[0], branch_cache[0]
    keys, values = k_cache[0], v_cache[0]
    width = tokens.shape[1]

    chunks = []
    picked = pick(tokens, blocks)
    ups, downs = [[p] for p in picked], [[p] for p in picked]
    for step in range(3):
        for slot in range(2):
            ups[slot].append(ring(ups[slot][-1], 1))
            downs[slot].append(ring(downs[slot][-1], -1))
    far = [ring(ups[0][3], 1), ring(downs[1][3], -1)]
    for slot in range(2):
        chunks += ups[slot] + [far[slot]] + downs[slot][:0:-1]

    qkv = w_qkv.reshape(w_qkv.shape[0], -1)
    qkv_other = swap(qkv)
    mlp_in_other = swap(w_mlp_in)

    stale_first, stale_second = pack_stale(keys, values, blocks)
    stale_x = [stale_first] + [along_x(stale_first, k) for k in range(1, SIDE)]
    stale_y = [stale_second] + [along_y(stale_second, k) for k in range(1, SIDE)]

    attn_out_other = swap(w_attn_out)
    mlp_out_other = swap(w_mlp_out)
    tokens_other = swap(tokens)
    cached_other = swap(cached)
    factor = jnp.where(core == 0, 1.0 - GUIDANCE, GUIDANCE).astype(F32)
    gate = (factor * modulation[0, 2]).reshape(HEAD, 1, width)
    gate_other = swap(gate)
    gate_here = lax.dynamic_index_in_dim(gate, z, 0, keepdims=False)
    gate_there = lax.dynamic_index_in_dim(gate_other, z, 0, keepdims=False)
    stale = (
        factor * tokens.astype(F32)
        + gate_here * cached.astype(F32)
        + (1.0 - factor) * tokens_other.astype(F32)
        + gate_there * cached_other.astype(F32)
    ).astype(BF16)

    message_x, message_y, rows = project(
        blocks,
        counts,
        where,
        chunks,
        modulation[0],
        qkv,
        qkv_other,
        q_gain.reshape(1, HDIM),
        k_gain.reshape(1, HDIM),
        keys,
        values,
    )
    fresh_x = [message_x] + [along_x(message_x, k) for k in range(1, SIDE)]
    fresh_y = [message_y] + [along_y(message_y, k) for k in range(1, SIDE)]

    units, units_send = hidden_units(where, rows, w_mlp_in, mlp_in_other)
    units_other = swap(units_send)
    base = out_product(
        units_out_kernel, F32, "units_out", where, units, units_other, w_mlp_out, mlp_out_other,
        gate, gate_other,
    )

    part_y, part_x = attend(stale_x, stale_y, fresh_x, fresh_y)
    parts = [part_y[0]] + [along_y(part_y[k], -k) for k in range(1, SIDE)]
    parts += [part_x[0]] + [along_x(part_x[k], -k) for k in range(1, SIDE)]
    attended, attended_send = join(where, parts)
    attended_other = swap(attended_send)
    sums = out_product(
        heads_out_kernel, BF16, "heads_out", where, attended, attended_other, w_attn_out,
        attn_out_other, gate, gate_other, base,
    )
    sums = lax.all_to_all(sums, "head", 0, 0, tiled=True)
    final = finish(where, sums, tokens, tokens_other, stale)
    final_other = swap(final)
    out = lax.dynamic_update_slice(stale, final, (own_slot * BLOCK, 0))
    return lax.dynamic_update_slice(out, final_other, (other_slot * BLOCK, 0))


def solution(mesh):
    in_specs = (
        P("branch", "seq", "head"),
        P("branch", None, None),
        P("branch", "seq", "head"),
        P("branch", "seq", "head"),
        P("branch", "seq", "head"),
        P("branch", None, "head"),
        P("branch", "head"),
        P("head", "branch"),
        P("head", "branch"),
        P(),
        P(),
        P("seq", None),
        P("seq"),
    )
    out_specs = P("seq", "head")
    return jax.shard_map(local, mesh=mesh, in_specs=in_specs, out_specs=out_specs, check_vma=False)
```

```python
import functools

import jax
import jax.numpy as jnp
from jax import lax
from jax.experimental import pallas as pl
from jax.experimental.pallas import tpu as pltpu
from jax.sharding import Mesh, PartitionSpec as P

HDIM = 128
BLOCK = 128
GUIDANCE = 1.5
EPSILON = 1e-06
LOG2E = 1.4426950408889634
HEAD = 8
SIDE = 4
STALE = 6
STAT_ROWS = 16
MIB = 1024 * 1024

F32 = jnp.float32
BF16 = jnp.bfloat16


def whole():
    return pl.BlockSpec(memory_space=pltpu.VMEM)


def scalars():
    return pl.BlockSpec(memory_space=pltpu.SMEM)


def in_hbm():
    return pl.BlockSpec(memory_space=pltpu.HBM)


def anywhere():
    return pl.BlockSpec(memory_space=pl.ANY)


def params(mebibytes=58):
    return pltpu.CompilerParams(vmem_limit_bytes=mebibytes * MIB)


def dot(left, right):
    return jnp.dot(left, right, preferred_element_type=F32)


def begin(pairs, arrived):
    copies = [
        pltpu.make_async_copy(source, target, arrived.at[i])
        for i, (source, target) in enumerate(pairs)
    ]
    for copy in copies:
        copy.start()
    return copies


def block_rows(number):
    return pl.ds(pl.multiple_of(number * BLOCK, BLOCK), BLOCK)


def pick_kernel(blocks_ref, counts_ref, tokens_ref, k_ref, v_ref, *refs):
    out_ref, packed, (stale_s, arrived, sent) = refs[0], refs[1:3], refs[3:]
    pairs = [
        (tokens_ref.at[block_rows(blocks_ref[0, j])], out_ref.at[pl.ds(j * BLOCK, BLOCK)])
        for j in range(2)
    ]
    low = jnp.minimum(blocks_ref[0, 0], blocks_ref[0, 1])
    high = jnp.maximum(blocks_ref[0, 0], blocks_ref[0, 1])
    for i in range(STALE):
        index = i + (i >= low).astype(jnp.int32)
        index = index + (index >= high).astype(jnp.int32)
        for half, ref in enumerate((k_ref, v_ref)):
            pairs.append((ref.at[block_rows(index)], stale_s.at[half, pl.ds(i * BLOCK, BLOCK)]))
    copies = begin(pairs, arrived)
    for copy in copies[2:]:
        copy.wait()
    pairs = [
        (stale_s.at[half, :, pl.ds(head * HDIM, HDIM)], packed[head].at[:, pl.ds(half * HDIM, HDIM)])
        for head in range(2)
        for half in range(2)
    ]
    for copy in copies[:2] + begin(pairs, sent):
        copy.wait()


def pick(tokens, keys, values, blocks, counts):
    shape = jax.ShapeDtypeStruct((2 * BLOCK, tokens.shape[1]), BF16)
    stale = jax.ShapeDtypeStruct((STALE * BLOCK, 2 * HDIM), BF16)
    return pl.pallas_call(
        pick_kernel,
        in_specs=[scalars(), scalars()] + [in_hbm()] * 3,
        out_specs=[whole()] + [in_hbm()] * 2,
        out_shape=[shape, stale, stale],
        scratch_shapes=[
            pltpu.VMEM((2, STALE * BLOCK, 2 * HDIM), BF16),
            pltpu.SemaphoreType.DMA((2 + 2 * STALE,)),
            pltpu.SemaphoreType.DMA((4,)),
        ],
        compiler_params=params(),
        name="pick",
    )(blocks, counts, tokens, keys, values)


def project_kernel(blocks_ref, counts_ref, *refs):
    sources = refs[: HEAD + 5]
    keys_ref, values_ref = refs[HEAD + 5 : HEAD + 7]
    x_ref, y_ref, rows_ref = refs[HEAD + 7 : HEAD + 10]
    chunk_s, mod_ref, own_ref, other_ref, q_gain_ref, k_gain_ref, old_s, arrived = refs[HEAD + 10 :]
    core = lax.axis_index("branch")
    z = lax.axis_index("head")
    old = block_rows(blocks_ref[0, 1])
    targets = [chunk_s.at[k] for k in range(HEAD)]
    targets += [mod_ref, own_ref, other_ref, q_gain_ref, k_gain_ref]
    pairs = list(zip(sources, targets))
    pairs += [(keys_ref.at[old], old_s.at[0]), (values_ref.at[old], old_s.at[1])]
    copies = begin(pairs, arrived)
    for copy in copies[: HEAD + 1]:
        copy.wait()
    width = chunk_s.shape[2]
    full = HEAD * width
    step = 32
    for row in range(0, 2 * BLOCK, step):
        values = [chunk_s[k, row : row + step, :].astype(F32) for k in range(HEAD)]
        mean = sum(jnp.sum(v, axis=-1, keepdims=True) for v in values) / full
        centred = [v - mean for v in values]
        var = sum(jnp.sum(c * c, axis=-1, keepdims=True) for c in centred) / full
        inverse = lax.rsqrt(var + EPSILON)
        for k in range(HEAD):
            owner = lax.rem(z - k + HEAD, HEAD)
            columns = pl.ds(pl.multiple_of(owner * width, width), width)
            shift = mod_ref[0, :, columns]
            scale = mod_ref[1, :, columns]
            rows_ref[row : row + step, columns] = (
                centred[k] * inverse * (1.0 + scale) + shift
            ).astype(BF16)
    for copy in copies[HEAD + 1 :]:
        copy.wait()
    half = full // 2
    here = pl.ds(pl.multiple_of(core * half, half), half)
    there = pl.ds(pl.multiple_of((1 - core) * half, half), half)
    query, key, value = (
        dot(rows_ref[:, here], own_ref[i]) + dot(rows_ref[:, there], other_ref[i]) for i in range(3)
    )

    def norm(values, gain_ref):
        power = jnp.mean(values * values, axis=-1, keepdims=True)
        return (values * lax.rsqrt(power + EPSILON) * gain_ref[...]).astype(BF16)

    live = counts_ref[0] > 1
    for head, fresh_ref, query_ref in ((0, x_ref, y_ref), (1, y_ref, x_ref)):
        at = head * HDIM
        query_ref[:, 2 * HDIM :] = norm(query[:, at : at + HDIM], q_gain_ref)
        new_key = norm(key[:, at : at + HDIM], k_gain_ref)
        new_value = value[:, at : at + HDIM].astype(BF16)
        fresh_ref[:BLOCK, :HDIM] = new_key[:BLOCK]
        fresh_ref[:BLOCK, HDIM : 2 * HDIM] = new_value[:BLOCK]
        fresh_ref[BLOCK:, :HDIM] = jnp.where(live, new_key[BLOCK:], old_s[0, :, at : at + HDIM])
        fresh_ref[BLOCK:, HDIM : 2 * HDIM] = jnp.where(
            live, new_value[BLOCK:], old_s[1, :, at : at + HDIM]
        )


def project(blocks, counts, chunks, mod, own, other, q_gain, k_gain, keys, values):
    rows, width = chunks[0].shape
    full = HEAD * width
    sources = [*chunks, mod, own, other, q_gain, k_gain, keys, values]
    return pl.pallas_call(
        project_kernel,
        in_specs=[scalars()] * 2 + [in_hbm()] * len(sources),
        out_specs=[whole()] * 3,
        out_shape=[
            jax.ShapeDtypeStruct((rows, 3 * HDIM), BF16),
            jax.ShapeDtypeStruct((rows, 3 * HDIM), BF16),
            jax.ShapeDtypeStruct((rows, full), BF16),
        ],
        scratch_shapes=[
            pltpu.VMEM((HEAD, rows, width), BF16),
            *[pltpu.VMEM(a.shape, a.dtype) for a in (mod, own, other, q_gain, k_gain)],
            pltpu.VMEM((2, BLOCK, 2 * HDIM), BF16),
            pltpu.SemaphoreType.DMA((len(sources),)),
        ],
        compiler_params=params(),
        cost_estimate=pl.CostEstimate(
            flops=2 * rows * full * 6 * HDIM, bytes_accessed=8 * MIB, transcendentals=0
        ),
        name="project",
    )(blocks, counts, *sources)


def hidden_kernel(rows_ref, own_ref, other_ref, mine_ref, theirs_ref):
    core = lax.axis_index("branch")
    half = own_ref.shape[0]
    here = pl.ds(pl.multiple_of(core * half, half), half)
    there = pl.ds(pl.multiple_of((1 - core) * half, half), half)
    total = dot(rows_ref[:, here], own_ref[...]) + dot(rows_ref[:, there], other_ref[...])
    active = jax.nn.gelu(total, approximate=True).astype(BF16)
    first = core == 0
    mine_ref[...] = jnp.where(first, active[:BLOCK], active[BLOCK:])
    theirs_ref[...] = jnp.where(first, active[BLOCK:], active[:BLOCK])


def hidden_units(rows, own, other):
    units = own.shape[1]
    shape = jax.ShapeDtypeStruct((BLOCK, units), BF16)
    return pl.pallas_call(
        hidden_kernel,
        in_specs=[whole()] * 3,
        out_specs=[whole()] * 2,
        out_shape=[shape, shape],
        compiler_params=params(14),
        cost_estimate=pl.CostEstimate(
            flops=2 * rows.shape[0] * rows.shape[1] * units,
            bytes_accessed=8 * MIB,
            transcendentals=rows.shape[0] * units,
        ),
        name="hidden_units",
    )(rows, own, other)


def gated(mine_ref, theirs_ref, w_own, w_other, mod_own, mod_other, emit):
    core = lax.axis_index("branch")
    factor = jnp.where(core == 0, 1.0 - GUIDANCE, GUIDANCE)
    width = w_own.shape[1] // (HEAD // 2)
    left = jnp.concatenate([mine_ref[...], theirs_ref[...]], axis=0)
    for weights, side in ((w_own, core), (w_other, 1 - core)):
        both = dot(left, weights[...])
        for i in range(HEAD // 2):
            part = both[:, i * width : (i + 1) * width]
            chunk = side * (HEAD // 2) + i
            columns = pl.ds(pl.multiple_of(chunk * width, width), width)
            gate_own = factor * mod_own[2, :, columns]
            gate_other = (1.0 - factor) * mod_other[2, :, columns]
            emit(chunk, part[:BLOCK] * gate_own + part[BLOCK:] * gate_other)


def units_out_kernel(mine_ref, theirs_ref, own_ref, other_ref, mod_ref, mod_other_ref, out_ref):
    def emit(chunk, value):
        out_ref[chunk] = value

    gated(mine_ref, theirs_ref, own_ref, other_ref, mod_ref, mod_other_ref, emit)


def heads_out_kernel(
    mine_ref, theirs_ref, own_ref, other_ref, mod_ref, mod_other_ref, base_ref, out_ref
):
    def emit(chunk, value):
        out_ref[chunk] = (base_ref[chunk] + value).astype(BF16)

    gated(mine_ref, theirs_ref, own_ref, other_ref, mod_ref, mod_other_ref, emit)


def out_product(kernel, dtype, name, limit, mine, theirs, own, other, mod, mod_other, *base):
    width = own.shape[1] // (HEAD // 2)
    return pl.pallas_call(
        kernel,
        in_specs=[whole()] * (6 + len(base)),
        out_specs=whole(),
        out_shape=jax.ShapeDtypeStruct((HEAD, BLOCK, width), dtype),
        compiler_params=params(limit),
        cost_estimate=pl.CostEstimate(
            flops=8 * BLOCK * own.shape[0] * own.shape[1],
            bytes_accessed=6 * MIB,
            transcendentals=0,
        ),
        name=name,
    )(mine, theirs, own, other, mod, mod_other, *base)


def attend_kernel(*refs):
    stale_ref = refs[0]
    fresh, asked = refs[1 : 1 + SIDE], refs[1 + SIDE : 1 + 2 * SIDE]
    outs = refs[-9:-5]
    key_s, score_s, query_s, stat_s, arrived = refs[-5:]
    rows = 2 * BLOCK
    keys = key_s.shape[0]
    tiles = 4
    piece = keys // tiles
    unit = LOG2E * HDIM**-0.5
    old = stale_ref.shape[0]
    pairs = [(asked[k].at[:, pl.ds(2 * HDIM, HDIM)], query_s.at[k]) for k in range(SIDE)]
    pairs += [
        (fresh[k].at[:, pl.ds(0, 2 * HDIM)], key_s.at[pl.ds(old + k * rows, rows)])
        for k in range(SIDE)
    ]
    pairs.append((stale_ref, key_s.at[pl.ds(0, old)]))
    for copy in begin(pairs, arrived):
        copy.wait()
    stat_s[...] = jnp.zeros_like(stat_s)

    def tile(index, carry):
        query = query_s[index]
        top = None
        for k in range(tiles):
            part = key_s[k * piece : (k + 1) * piece, :HDIM]
            scores = lax.dot_general(
                query, part, (((1,), (1,)), ((), ())), preferred_element_type=F32
            )
            score_s[:, k * piece : (k + 1) * piece] = scores
            here = jnp.max(scores, axis=-1, keepdims=True)
            top = here if top is None else jnp.maximum(top, here)
        top = top * unit
        total = jnp.zeros((rows, 1), F32)
        summed = jnp.zeros((rows, HDIM), F32)
        for k in range(tiles):
            weights = jnp.exp2(score_s[:, k * piece : (k + 1) * piece] * unit - top)
            total = total + jnp.sum(weights, axis=-1, keepdims=True)
            summed = summed + dot(
                weights.astype(BF16), key_s[k * piece : (k + 1) * piece, HDIM:]
            )
        query_s[index] = (summed / total).astype(BF16)
        lane = lax.broadcasted_iota(jnp.int32, (rows, HDIM), 1)
        stat_s[...] = jnp.where(lane == index, top + jnp.log2(total), stat_s[...])
        return carry

    lax.fori_loop(0, SIDE, tile, 0)
    stats = jnp.transpose(stat_s[...])
    for index in range(SIDE):
        outs[index][:rows, :] = query_s[index]
        row = stats[index : index + 1, :]
        high = row.astype(BF16).astype(F32)
        middle = (row - high).astype(BF16).astype(F32)
        low = row - high - middle
        parts = [p[:, at : at + HDIM] for p in (high, middle, low) for at in (0, HDIM)]
        parts.append(jnp.zeros((STAT_ROWS - 6, HDIM), F32))
        outs[index][rows:, :] = jnp.concatenate(parts, axis=0).astype(BF16)


def attend(stale, fresh, asked, early, name):
    rows = 2 * BLOCK
    keys = SIDE * (STALE + 2) * BLOCK
    shape = jax.ShapeDtypeStruct((rows + STAT_ROWS, HDIM), BF16)
    return pl.pallas_call(
        attend_kernel,
        in_specs=[in_hbm()] * (1 + 2 * SIDE) + [anywhere()] * len(early),
        out_specs=[whole()] * SIDE,
        out_shape=[shape] * SIDE,
        scratch_shapes=[
            pltpu.VMEM((keys, 2 * HDIM), BF16),
            pltpu.VMEM((rows, keys), F32),
            pltpu.VMEM((SIDE, rows, HDIM), BF16),
            pltpu.VMEM((rows, HDIM), F32),
            pltpu.SemaphoreType.DMA((1 + 2 * SIDE,)),
        ],
        compiler_params=params(),
        cost_estimate=pl.CostEstimate(
            flops=4 * SIDE * rows * keys * HDIM,
            bytes_accessed=4 * MIB,
            transcendentals=SIDE * rows * keys,
        ),
        name=name,
    )(stale, *fresh, *asked, *early)


def join_kernel(*refs):
    parts, (mine_ref, theirs_ref) = refs[:8], refs[8:]
    rows = 2 * BLOCK
    stats = []
    for part in parts:
        tail = part[rows:, :].astype(F32)
        joined = [jnp.concatenate([tail[i : i + 1], tail[i + 1 : i + 2]], axis=1) for i in (0, 2, 4)]
        stats.append(joined[0] + joined[1] + joined[2])
    stats = jnp.concatenate(stats + [jnp.zeros((HDIM - 2 * SIDE, rows), F32)], axis=0)
    columns = jnp.transpose(stats)
    first = lax.axis_index("branch") == 0
    for head in range(2):
        level = [columns[:, head * SIDE + k : head * SIDE + k + 1] for k in range(SIDE)]
        top = functools.reduce(jnp.maximum, level)
        shares = [jnp.exp2(value - top) for value in level]
        inverse = 1.0 / sum(shares)
        result = sum(
            (shares[k] * inverse) * parts[head * SIDE + k][:rows, :].astype(F32)
            for k in range(SIDE)
        ).astype(BF16)
        at = slice(head * HDIM, (head + 1) * HDIM)
        mine_ref[:, at] = jnp.where(first, result[:BLOCK], result[BLOCK:])
        theirs_ref[:, at] = jnp.where(first, result[BLOCK:], result[:BLOCK])


def join(parts):
    shape = jax.ShapeDtypeStruct((BLOCK, 2 * HDIM), BF16)
    return pl.pallas_call(
        join_kernel,
        in_specs=[whole()] * 8,
        out_specs=[whole()] * 2,
        out_shape=[shape, shape],
        compiler_params=params(4),
        name="join",
    )(*parts)


def stale_kernel(
    blocks_ref, mod_ref, mod_other_ref, own_ref, other_ref, cached_ref, cached_other_ref, out_ref,
    kept_ref, old_ref,
):
    core = lax.axis_index("branch")
    factor = jnp.where(core == 0, 1.0 - GUIDANCE, GUIDANCE)
    width = own_ref.shape[1]
    columns = pl.ds(pl.multiple_of(lax.axis_index("head") * width, width), width)
    gate = factor * mod_ref[2, :, columns]
    gate_other = (1.0 - factor) * mod_other_ref[2, :, columns]
    out_ref[...] = (
        factor * own_ref[...].astype(F32)
        + gate * cached_ref[...].astype(F32)
        + (1.0 - factor) * other_ref[...].astype(F32)
        + gate_other * cached_other_ref[...].astype(F32)
    ).astype(BF16)
    rows = block_rows(jnp.where(core == 0, blocks_ref[0, 0], blocks_ref[0, 1]))
    kept_ref[...] = factor * own_ref[rows, :].astype(F32) + (1.0 - factor) * other_ref[
        rows, :
    ].astype(F32)
    old_ref[...] = out_ref[rows, :]


def stale_rows(blocks, mod, mod_other, own, other, cached, cached_other):
    rows, width = own.shape
    return pl.pallas_call(
        stale_kernel,
        in_specs=[scalars()] + [whole()] * 6,
        out_specs=[whole()] * 3,
        out_shape=[
            jax.ShapeDtypeStruct((rows, width), BF16),
            jax.ShapeDtypeStruct((BLOCK, width), F32),
            jax.ShapeDtypeStruct((BLOCK, width), BF16),
        ],
        compiler_params=params(8),
        name="stale_rows",
    )(blocks, mod, mod_other, own, other, cached, cached_other)


def finish_kernel(counts_ref, parts_ref, kept_ref, old_ref, out_ref):
    total = kept_ref[...]
    for k in range(HEAD):
        total = total + parts_ref[k].astype(F32)
    live = lax.axis_index("branch") < counts_ref[0]
    out_ref[...] = jnp.where(live, total.astype(BF16), old_ref[...])


def finish(counts, parts, kept, old):
    return pl.pallas_call(
        finish_kernel,
        in_specs=[scalars()] + [whole()] * 3,
        out_specs=whole(),
        out_shape=jax.ShapeDtypeStruct(old.shape, BF16),
        compiler_params=params(4),
        name="finish",
    )(counts, parts, kept, old)


def place_kernel(blocks_ref, stale_ref, own_ref, other_ref, out_ref, sent):
    core = lax.axis_index("branch")
    copies = []
    for i, ref in enumerate((own_ref, other_ref)):
        first = core == i
        slot = jnp.where(first, blocks_ref[0, 0], blocks_ref[0, 1])
        copies.append(pltpu.make_async_copy(ref, out_ref.at[block_rows(slot)], sent.at[i]))
    for copy in copies:
        copy.start()
    for copy in copies:
        copy.wait()


def place(blocks, stale, own, other):
    return pl.pallas_call(
        place_kernel,
        in_specs=[scalars(), in_hbm(), whole(), whole()],
        out_specs=in_hbm(),
        out_shape=jax.ShapeDtypeStruct(stale.shape, BF16),
        scratch_shapes=[pltpu.SemaphoreType.DMA((2,))],
        input_output_aliases={1: 0},
        compiler_params=params(2),
        name="place",
    )(blocks, stale, own, other)


def ring(array, shift):
    return lax.ppermute(array, "head", [(i, (i + shift) % HEAD) for i in range(HEAD)])


def swap(array):
    return lax.ppermute(array, "branch", [(0, 1), (1, 0)])


def along(axis, array, shift):
    return lax.ppermute(array, axis, [(i, (i + shift) % SIDE) for i in range(SIDE)])


def local(
    hidden,
    modulation,
    branch_cache,
    k_cache,
    v_cache,
    w_qkv,
    w_mlp_in,
    w_attn_out,
    w_mlp_out,
    q_gain,
    k_gain,
    blocks,
    counts,
):
    tokens, cached = hidden[0], branch_cache[0]
    keys, values = k_cache[0], v_cache[0]
    mod = jnp.transpose(modulation, (1, 0, 2))

    picked, stale_first, stale_second = pick(tokens, keys, values, blocks, counts)
    ups, downs = [picked], [picked]
    for step in range(3):
        ups.append(ring(ups[-1], 1))
        downs.append(ring(downs[-1], -1))
    chunks = ups + [ring(ups[-1], 1)] + downs[:0:-1]

    stale_x = lax.all_gather(stale_first, "x", axis=0, tiled=True)
    stale_y = lax.all_gather(stale_second, "y", axis=0, tiled=True)

    qkv = jnp.transpose(w_qkv, (1, 0, 2))
    qkv_other = swap(qkv)
    mod_other = swap(mod)
    mlp_in_other = swap(w_mlp_in)
    mlp_out_other = swap(w_mlp_out)
    attn_out_other = swap(w_attn_out)
    tokens_other = swap(tokens)
    cached_other = swap(cached)

    message_x, message_y, rows = project(
        blocks,
        counts,
        chunks,
        mod,
        qkv,
        qkv_other,
        q_gain.reshape(1, HDIM),
        k_gain.reshape(1, HDIM),
        keys,
        values,
    )
    fresh_x = [message_x] + [along("x", message_x, k) for k in range(1, SIDE)]
    fresh_y = [message_y] + [along("y", message_y, k) for k in range(1, SIDE)]

    units, units_send = hidden_units(rows, w_mlp_in, mlp_in_other)
    units_other = swap(units_send)
    base = out_product(
        units_out_kernel, F32, "units_out", 14, units, units_other, w_mlp_out, mlp_out_other,
        mod, mod_other,
    )

    part_y = attend(stale_x, fresh_x, fresh_y, [base], "attend_first")
    part_x = attend(stale_y, fresh_y, fresh_x, [part_y[0]], "attend_second")
    parts = [part_y[0]] + [along("y", part_y[k], -k) for k in range(1, SIDE)]
    parts += [part_x[0]] + [along("x", part_x[k], -k) for k in range(1, SIDE)]
    attended, attended_send = join(parts)
    attended_other = swap(attended_send)
    sums = out_product(
        heads_out_kernel, BF16, "heads_out", 10, attended, attended_other, w_attn_out,
        attn_out_other, mod, mod_other, base,
    )
    sums = lax.all_to_all(sums, "head", 0, 0, tiled=True)
    stale, kept, old = stale_rows(
        blocks, mod, mod_other, tokens, tokens_other, cached, cached_other
    )
    final = finish(counts, sums, kept, old)
    return place(blocks, stale, final, swap(final))


def solution(mesh):
    mesh = Mesh(mesh.devices.reshape(2, HEAD, SIDE, SIDE), ("branch", "head", "y", "x"))
    seq = ("y", "x")
    in_specs = (
        P("branch", seq, "head"),
        P("branch", None, None),
        P("branch", seq, "head"),
        P("branch", seq, "head"),
        P("branch", seq, "head"),
        P("branch", None, "head"),
        P("branch", "head"),
        P("head", "branch"),
        P("head", "branch"),
        P(),
        P(),
        P(seq, None),
        P(seq),
    )
    out_specs = P(seq, "head")
    return jax.shard_map(local, mesh=mesh, in_specs=in_specs, out_specs=out_specs, check_vma=False)
```

```python
import functools

import jax
import jax.numpy as jnp
from jax import lax
from jax.experimental import pallas as pl
from jax.experimental.pallas import tpu as pltpu
from jax.sharding import Mesh, PartitionSpec as P

HDIM = 128
BLOCK = 128
GUIDANCE = 1.5
EPSILON = 1e-06
LOG2E = 1.4426950408889634
HEAD = 8
SIDE = 4
STALE = 6
STAT_ROWS = 16
MIB = 1024 * 1024

F32 = jnp.float32
BF16 = jnp.bfloat16


def whole():
    return pl.BlockSpec(memory_space=pltpu.VMEM)


def scalars():
    return pl.BlockSpec(memory_space=pltpu.SMEM)


def in_hbm():
    return pl.BlockSpec(memory_space=pltpu.HBM)


def anywhere():
    return pl.BlockSpec(memory_space=pl.ANY)


def params(mebibytes=58):
    return pltpu.CompilerParams(vmem_limit_bytes=mebibytes * MIB)


def dot(left, right):
    return jnp.dot(left, right, preferred_element_type=F32)


def begin(pairs, arrived):
    copies = [
        pltpu.make_async_copy(source, target, arrived.at[i])
        for i, (source, target) in enumerate(pairs)
    ]
    for copy in copies:
        copy.start()
    return copies


def block_rows(number):
    return pl.ds(pl.multiple_of(number * BLOCK, BLOCK), BLOCK)


def pick_kernel(blocks_ref, counts_ref, tokens_ref, k_ref, v_ref, *refs):
    out_ref, packed, (stale_s, arrived, sent) = refs[0], refs[1:3], refs[3:]
    pairs = [
        (tokens_ref.at[block_rows(blocks_ref[0, j])], out_ref.at[pl.ds(j * BLOCK, BLOCK)])
        for j in range(2)
    ]
    low = jnp.minimum(blocks_ref[0, 0], blocks_ref[0, 1])
    high = jnp.maximum(blocks_ref[0, 0], blocks_ref[0, 1])
    for i in range(STALE):
        index = i + (i >= low).astype(jnp.int32)
        index = index + (index >= high).astype(jnp.int32)
        for half, ref in enumerate((k_ref, v_ref)):
            pairs.append((ref.at[block_rows(index)], stale_s.at[half, pl.ds(i * BLOCK, BLOCK)]))
    copies = begin(pairs, arrived)
    for copy in copies[2:]:
        copy.wait()
    pairs = [
        (stale_s.at[half, :, pl.ds(head * HDIM, HDIM)], packed[head].at[:, pl.ds(half * HDIM, HDIM)])
        for head in range(2)
        for half in range(2)
    ]
    for copy in copies[:2] + begin(pairs, sent):
        copy.wait()


def pick(tokens, keys, values, blocks, counts):
    shape = jax.ShapeDtypeStruct((2 * BLOCK, tokens.shape[1]), BF16)
    stale = jax.ShapeDtypeStruct((STALE * BLOCK, 2 * HDIM), BF16)
    return pl.pallas_call(
        pick_kernel,
        in_specs=[scalars(), scalars()] + [in_hbm()] * 3,
        out_specs=[whole()] + [in_hbm()] * 2,
        out_shape=[shape, stale, stale],
        scratch_shapes=[
            pltpu.VMEM((2, STALE * BLOCK, 2 * HDIM), BF16),
            pltpu.SemaphoreType.DMA((2 + 2 * STALE,)),
            pltpu.SemaphoreType.DMA((4,)),
        ],
        compiler_params=params(),
        name="pick",
    )(blocks, counts, tokens, keys, values)


def project_kernel(blocks_ref, counts_ref, *refs):
    sources = refs[: HEAD + 5]
    keys_ref, values_ref = refs[HEAD + 5 : HEAD + 7]
    x_ref, y_ref, asked_ref, rows_ref = refs[HEAD + 7 : HEAD + 11]
    chunk_s, mod_ref, own_ref, other_ref, q_gain_ref, k_gain_ref, old_s, arrived = refs[HEAD + 11 :]
    core = lax.axis_index("branch")
    z = lax.axis_index("head")
    old = block_rows(blocks_ref[0, 1])
    targets = [chunk_s.at[k] for k in range(HEAD)]
    targets += [mod_ref, own_ref, other_ref, q_gain_ref, k_gain_ref]
    pairs = list(zip(sources, targets))
    pairs += [(keys_ref.at[old], old_s.at[0]), (values_ref.at[old], old_s.at[1])]
    copies = begin(pairs, arrived)
    for copy in copies[: HEAD + 1]:
        copy.wait()
    width = chunk_s.shape[2]
    full = HEAD * width
    step = 32
    for row in range(0, 2 * BLOCK, step):
        values = [chunk_s[k, row : row + step, :].astype(F32) for k in range(HEAD)]
        mean = sum(jnp.sum(v, axis=-1, keepdims=True) for v in values) / full
        centred = [v - mean for v in values]
        var = sum(jnp.sum(c * c, axis=-1, keepdims=True) for c in centred) / full
        inverse = lax.rsqrt(var + EPSILON)
        for k in range(HEAD):
            owner = lax.rem(z - k + HEAD, HEAD)
            columns = pl.ds(pl.multiple_of(owner * width, width), width)
            shift = mod_ref[0, :, columns]
            scale = mod_ref[1, :, columns]
            rows_ref[row : row + step, columns] = (
                centred[k] * inverse * (1.0 + scale) + shift
            ).astype(BF16)
    for copy in copies[HEAD + 1 :]:
        copy.wait()
    half = full // 2
    here = pl.ds(pl.multiple_of(core * half, half), half)
    there = pl.ds(pl.multiple_of((1 - core) * half, half), half)
    query, key, value = (
        dot(rows_ref[:, here], own_ref[i]) + dot(rows_ref[:, there], other_ref[i]) for i in range(3)
    )

    def norm(values, gain_ref):
        power = jnp.mean(values * values, axis=-1, keepdims=True)
        return (values * lax.rsqrt(power + EPSILON) * gain_ref[...]).astype(BF16)

    live = counts_ref[0] > 1
    asked_ref[...] = norm(query[:, :HDIM], q_gain_ref)
    x_ref[:, 2 * HDIM :] = norm(query[:, HDIM:], q_gain_ref)
    for head, fresh_ref in ((0, x_ref), (1, y_ref)):
        at = head * HDIM
        new_key = norm(key[:, at : at + HDIM], k_gain_ref)
        new_value = value[:, at : at + HDIM].astype(BF16)
        fresh_ref[:BLOCK, :HDIM] = new_key[:BLOCK]
        fresh_ref[:BLOCK, HDIM : 2 * HDIM] = new_value[:BLOCK]
        fresh_ref[BLOCK:, :HDIM] = jnp.where(live, new_key[BLOCK:], old_s[0, :, at : at + HDIM])
        fresh_ref[BLOCK:, HDIM : 2 * HDIM] = jnp.where(
            live, new_value[BLOCK:], old_s[1, :, at : at + HDIM]
        )


def project(blocks, counts, chunks, mod, own, other, q_gain, k_gain, keys, values):
    rows, width = chunks[0].shape
    full = HEAD * width
    sources = [*chunks, mod, own, other, q_gain, k_gain, keys, values]
    return pl.pallas_call(
        project_kernel,
        in_specs=[scalars()] * 2 + [in_hbm()] * len(sources),
        out_specs=[whole()] * 4,
        out_shape=[
            jax.ShapeDtypeStruct((rows, 3 * HDIM), BF16),
            jax.ShapeDtypeStruct((rows, 2 * HDIM), BF16),
            jax.ShapeDtypeStruct((rows, HDIM), BF16),
            jax.ShapeDtypeStruct((rows, full), BF16),
        ],
        scratch_shapes=[
            pltpu.VMEM((HEAD, rows, width), BF16),
            *[pltpu.VMEM(a.shape, a.dtype) for a in (mod, own, other, q_gain, k_gain)],
            pltpu.VMEM((2, BLOCK, 2 * HDIM), BF16),
            pltpu.SemaphoreType.DMA((len(sources),)),
        ],
        compiler_params=params(),
        cost_estimate=pl.CostEstimate(
            flops=2 * rows * full * 6 * HDIM, bytes_accessed=8 * MIB, transcendentals=0
        ),
        name="project",
    )(blocks, counts, *sources)


def hidden_kernel(rows_ref, own_ref, other_ref, mine_ref, theirs_ref):
    core = lax.axis_index("branch")
    half = own_ref.shape[0]
    here = pl.ds(pl.multiple_of(core * half, half), half)
    there = pl.ds(pl.multiple_of((1 - core) * half, half), half)
    total = dot(rows_ref[:, here], own_ref[...]) + dot(rows_ref[:, there], other_ref[...])
    active = jax.nn.gelu(total, approximate=True).astype(BF16)
    first = core == 0
    mine_ref[...] = jnp.where(first, active[:BLOCK], active[BLOCK:])
    theirs_ref[...] = jnp.where(first, active[BLOCK:], active[:BLOCK])


def hidden_units(rows, own, other):
    units = own.shape[1]
    shape = jax.ShapeDtypeStruct((BLOCK, units), BF16)
    return pl.pallas_call(
        hidden_kernel,
        in_specs=[whole()] * 3,
        out_specs=[whole()] * 2,
        out_shape=[shape, shape],
        compiler_params=params(14),
        cost_estimate=pl.CostEstimate(
            flops=2 * rows.shape[0] * rows.shape[1] * units,
            bytes_accessed=8 * MIB,
            transcendentals=rows.shape[0] * units,
        ),
        name="hidden_units",
    )(rows, own, other)


def gated(mine_ref, theirs_ref, w_own, w_other, mod_own, mod_other, emit):
    core = lax.axis_index("branch")
    factor = jnp.where(core == 0, 1.0 - GUIDANCE, GUIDANCE)
    width = w_own.shape[1] // (HEAD // 2)
    left = jnp.concatenate([mine_ref[...], theirs_ref[...]], axis=0)
    for weights, side in ((w_own, core), (w_other, 1 - core)):
        both = dot(left, weights[...])
        for i in range(HEAD // 2):
            part = both[:, i * width : (i + 1) * width]
            chunk = side * (HEAD // 2) + i
            columns = pl.ds(pl.multiple_of(chunk * width, width), width)
            gate_own = factor * mod_own[2, :, columns]
            gate_other = (1.0 - factor) * mod_other[2, :, columns]
            emit(chunk, part[:BLOCK] * gate_own + part[BLOCK:] * gate_other)


def units_out_kernel(mine_ref, theirs_ref, own_ref, other_ref, mod_ref, mod_other_ref, out_ref):
    def emit(chunk, value):
        out_ref[chunk] = value

    gated(mine_ref, theirs_ref, own_ref, other_ref, mod_ref, mod_other_ref, emit)


def heads_out_kernel(
    mine_ref, theirs_ref, own_ref, other_ref, mod_ref, mod_other_ref, base_ref, out_ref
):
    def emit(chunk, value):
        out_ref[chunk] = (base_ref[chunk] + value).astype(BF16)

    gated(mine_ref, theirs_ref, own_ref, other_ref, mod_ref, mod_other_ref, emit)


def out_product(kernel, dtype, name, limit, mine, theirs, own, other, mod, mod_other, *base):
    width = own.shape[1] // (HEAD // 2)
    return pl.pallas_call(
        kernel,
        in_specs=[whole()] * (6 + len(base)),
        out_specs=whole(),
        out_shape=jax.ShapeDtypeStruct((HEAD, BLOCK, width), dtype),
        compiler_params=params(limit),
        cost_estimate=pl.CostEstimate(
            flops=8 * BLOCK * own.shape[0] * own.shape[1],
            bytes_accessed=6 * MIB,
            transcendentals=0,
        ),
        name=name,
    )(mine, theirs, own, other, mod, mod_other, *base)


def attend_kernel(*refs):
    stale_ref = refs[0]
    fresh, asked = refs[1 : 1 + SIDE], refs[1 + SIDE : 1 + 2 * SIDE]
    outs = refs[-9:-5]
    key_s, score_s, query_s, stat_s, arrived = refs[-5:]
    rows = 2 * BLOCK
    keys = key_s.shape[0]
    tiles = 4
    piece = keys // tiles
    unit = LOG2E * HDIM**-0.5
    old = stale_ref.shape[0]
    pairs = [
        (ref.at[:, pl.ds(ref.shape[1] - HDIM, HDIM)], query_s.at[k]) for k, ref in enumerate(asked)
    ]
    pairs += [
        (fresh[k].at[:, pl.ds(0, 2 * HDIM)], key_s.at[pl.ds(old + k * rows, rows)])
        for k in range(SIDE)
    ]
    pairs.append((stale_ref, key_s.at[pl.ds(0, old)]))
    for copy in begin(pairs, arrived):
        copy.wait()
    stat_s[...] = jnp.zeros_like(stat_s)

    def tile(index, carry):
        query = query_s[index]
        top = None
        for k in range(tiles):
            part = key_s[k * piece : (k + 1) * piece, :HDIM]
            scores = lax.dot_general(
                query, part, (((1,), (1,)), ((), ())), preferred_element_type=F32
            )
            score_s[:, k * piece : (k + 1) * piece] = scores
            here = jnp.max(scores, axis=-1, keepdims=True)
            top = here if top is None else jnp.maximum(top, here)
        top = top * unit
        total = jnp.zeros((rows, 1), F32)
        summed = jnp.zeros((rows, HDIM), F32)
        for k in range(tiles):
            weights = jnp.exp2(score_s[:, k * piece : (k + 1) * piece] * unit - top)
            total = total + jnp.sum(weights, axis=-1, keepdims=True)
            summed = summed + dot(
                weights.astype(BF16), key_s[k * piece : (k + 1) * piece, HDIM:]
            )
        query_s[index] = (summed / total).astype(BF16)
        lane = lax.broadcasted_iota(jnp.int32, (rows, HDIM), 1)
        stat_s[...] = jnp.where(lane == index, top + jnp.log2(total), stat_s[...])
        return carry

    lax.fori_loop(0, SIDE, tile, 0)
    stats = jnp.transpose(stat_s[...])
    for index in range(SIDE):
        outs[index][:rows, :] = query_s[index]
        row = stats[index : index + 1, :]
        high = row.astype(BF16).astype(F32)
        middle = (row - high).astype(BF16).astype(F32)
        low = row - high - middle
        parts = [p[:, at : at + HDIM] for p in (high, middle, low) for at in (0, HDIM)]
        parts.append(jnp.zeros((STAT_ROWS - 6, HDIM), F32))
        outs[index][rows:, :] = jnp.concatenate(parts, axis=0).astype(BF16)


def attend(stale, fresh, asked, early, name):
    rows = 2 * BLOCK
    keys = SIDE * (STALE + 2) * BLOCK
    shape = jax.ShapeDtypeStruct((rows + STAT_ROWS, HDIM), BF16)
    return pl.pallas_call(
        attend_kernel,
        in_specs=[in_hbm()] * (1 + 2 * SIDE) + [anywhere()] * len(early),
        out_specs=[whole()] * SIDE,
        out_shape=[shape] * SIDE,
        scratch_shapes=[
            pltpu.VMEM((keys, 2 * HDIM), BF16),
            pltpu.VMEM((rows, keys), F32),
            pltpu.VMEM((SIDE, rows, HDIM), BF16),
            pltpu.VMEM((rows, HDIM), F32),
            pltpu.SemaphoreType.DMA((1 + 2 * SIDE,)),
        ],
        compiler_params=params(),
        cost_estimate=pl.CostEstimate(
            flops=4 * SIDE * rows * keys * HDIM,
            bytes_accessed=4 * MIB,
            transcendentals=SIDE * rows * keys,
        ),
        name=name,
    )(stale, *fresh, *asked, *early)


def join_kernel(*refs):
    parts, (mine_ref, theirs_ref) = refs[:8], refs[8:]
    rows = 2 * BLOCK
    stats = []
    for part in parts:
        tail = part[rows:, :].astype(F32)
        joined = [jnp.concatenate([tail[i : i + 1], tail[i + 1 : i + 2]], axis=1) for i in (0, 2, 4)]
        stats.append(joined[0] + joined[1] + joined[2])
    stats = jnp.concatenate(stats + [jnp.zeros((HDIM - 2 * SIDE, rows), F32)], axis=0)
    columns = jnp.transpose(stats)
    first = lax.axis_index("branch") == 0
    for head in range(2):
        level = [columns[:, head * SIDE + k : head * SIDE + k + 1] for k in range(SIDE)]
        top = functools.reduce(jnp.maximum, level)
        shares = [jnp.exp2(value - top) for value in level]
        inverse = 1.0 / sum(shares)
        result = sum(
            (shares[k] * inverse) * parts[head * SIDE + k][:rows, :].astype(F32)
            for k in range(SIDE)
        ).astype(BF16)
        at = slice(head * HDIM, (head + 1) * HDIM)
        mine_ref[:, at] = jnp.where(first, result[:BLOCK], result[BLOCK:])
        theirs_ref[:, at] = jnp.where(first, result[BLOCK:], result[:BLOCK])


def join(parts):
    shape = jax.ShapeDtypeStruct((BLOCK, 2 * HDIM), BF16)
    return pl.pallas_call(
        join_kernel,
        in_specs=[whole()] * 8,
        out_specs=[whole()] * 2,
        out_shape=[shape, shape],
        compiler_params=params(4),
        name="join",
    )(*parts)


def stale_kernel(
    blocks_ref, mod_ref, mod_other_ref, own_ref, other_ref, cached_ref, cached_other_ref, out_ref,
    kept_ref, old_ref,
):
    core = lax.axis_index("branch")
    factor = jnp.where(core == 0, 1.0 - GUIDANCE, GUIDANCE)
    width = own_ref.shape[1]
    columns = pl.ds(pl.multiple_of(lax.axis_index("head") * width, width), width)
    gate = factor * mod_ref[2, :, columns]
    gate_other = (1.0 - factor) * mod_other_ref[2, :, columns]
    out_ref[...] = (
        factor * own_ref[...].astype(F32)
        + gate * cached_ref[...].astype(F32)
        + (1.0 - factor) * other_ref[...].astype(F32)
        + gate_other * cached_other_ref[...].astype(F32)
    ).astype(BF16)
    rows = block_rows(jnp.where(core == 0, blocks_ref[0, 0], blocks_ref[0, 1]))
    kept_ref[...] = factor * own_ref[rows, :].astype(F32) + (1.0 - factor) * other_ref[
        rows, :
    ].astype(F32)
    old_ref[...] = out_ref[rows, :]


def stale_rows(blocks, mod, mod_other, own, other, cached, cached_other):
    rows, width = own.shape
    return pl.pallas_call(
        stale_kernel,
        in_specs=[scalars()] + [whole()] * 6,
        out_specs=[whole()] * 3,
        out_shape=[
            jax.ShapeDtypeStruct((rows, width), BF16),
            jax.ShapeDtypeStruct((BLOCK, width), F32),
            jax.ShapeDtypeStruct((BLOCK, width), BF16),
        ],
        compiler_params=params(8),
        name="stale_rows",
    )(blocks, mod, mod_other, own, other, cached, cached_other)


def finish_kernel(counts_ref, parts_ref, kept_ref, old_ref, out_ref):
    total = kept_ref[...]
    for k in range(HEAD):
        total = total + parts_ref[k].astype(F32)
    live = lax.axis_index("branch") < counts_ref[0]
    out_ref[...] = jnp.where(live, total.astype(BF16), old_ref[...])


def finish(counts, parts, kept, old):
    return pl.pallas_call(
        finish_kernel,
        in_specs=[scalars()] + [whole()] * 3,
        out_specs=whole(),
        out_shape=jax.ShapeDtypeStruct(old.shape, BF16),
        compiler_params=params(4),
        name="finish",
    )(counts, parts, kept, old)


def place_kernel(blocks_ref, stale_ref, own_ref, other_ref, out_ref, sent):
    core = lax.axis_index("branch")
    copies = []
    for i, ref in enumerate((own_ref, other_ref)):
        first = core == i
        slot = jnp.where(first, blocks_ref[0, 0], blocks_ref[0, 1])
        copies.append(pltpu.make_async_copy(ref, out_ref.at[block_rows(slot)], sent.at[i]))
    for copy in copies:
        copy.start()
    for copy in copies:
        copy.wait()


def place(blocks, stale, own, other):
    return pl.pallas_call(
        place_kernel,
        in_specs=[scalars(), in_hbm(), whole(), whole()],
        out_specs=in_hbm(),
        out_shape=jax.ShapeDtypeStruct(stale.shape, BF16),
        scratch_shapes=[pltpu.SemaphoreType.DMA((2,))],
        input_output_aliases={1: 0},
        compiler_params=params(2),
        name="place",
    )(blocks, stale, own, other)


def ring(array, shift):
    return lax.ppermute(array, "head", [(i, (i + shift) % HEAD) for i in range(HEAD)])


def swap(array):
    return lax.ppermute(array, "branch", [(0, 1), (1, 0)])


def along(axis, array, shift):
    return lax.ppermute(array, axis, [(i, (i + shift) % SIDE) for i in range(SIDE)])


def local(
    hidden,
    modulation,
    branch_cache,
    k_cache,
    v_cache,
    w_qkv,
    w_mlp_in,
    w_attn_out,
    w_mlp_out,
    q_gain,
    k_gain,
    blocks,
    counts,
):
    tokens, cached = hidden[0], branch_cache[0]
    keys, values = k_cache[0], v_cache[0]
    mod = jnp.transpose(modulation, (1, 0, 2))

    picked, stale_first, stale_second = pick(tokens, keys, values, blocks, counts)
    ups, downs = [picked], [picked]
    for step in range(3):
        ups.append(ring(ups[-1], 1))
        downs.append(ring(downs[-1], -1))
    chunks = ups + [ring(ups[-1], 1)] + downs[:0:-1]

    stale_x = lax.all_gather(stale_first, "x", axis=0, tiled=True)
    stale_y = lax.all_gather(stale_second, "y", axis=0, tiled=True)

    qkv = jnp.transpose(w_qkv, (1, 0, 2))
    qkv_other = swap(qkv)
    mod_other = swap(mod)
    mlp_in_other = swap(w_mlp_in)
    mlp_out_other = swap(w_mlp_out)
    attn_out_other = swap(w_attn_out)
    tokens_other = swap(tokens)
    cached_other = swap(cached)

    message_x, message_y, asked, rows = project(
        blocks,
        counts,
        chunks,
        mod,
        qkv,
        qkv_other,
        q_gain.reshape(1, HDIM),
        k_gain.reshape(1, HDIM),
        keys,
        values,
    )
    fresh_x = [message_x] + [along("x", message_x, k) for k in range(1, SIDE)]
    asked_y = [asked] + [along("y", asked, k) for k in range(1, SIDE)]
    fresh_y = [message_y] + [along("y", message_y, k) for k in range(1, SIDE)]

    units, units_send = hidden_units(rows, w_mlp_in, mlp_in_other)
    units_other = swap(units_send)
    base = out_product(
        units_out_kernel, F32, "units_out", 14, units, units_other, w_mlp_out, mlp_out_other,
        mod, mod_other,
    )

    part_y = attend(stale_x, fresh_x, asked_y, [base], "attend_first")
    part_x = attend(stale_y, fresh_y, fresh_x, [part_y[0]], "attend_second")
    parts = [part_y[0]] + [along("y", part_y[k], -k) for k in range(1, SIDE)]
    parts += [part_x[0]] + [along("x", part_x[k], -k) for k in range(1, SIDE)]
    attended, attended_send = join(parts)
    attended_other = swap(attended_send)
    sums = out_product(
        heads_out_kernel, BF16, "heads_out", 10, attended, attended_other, w_attn_out,
        attn_out_other, mod, mod_other, base,
    )
    sums = lax.all_to_all(sums, "head", 0, 0, tiled=True)
    stale, kept, old = stale_rows(
        blocks, mod, mod_other, tokens, tokens_other, cached, cached_other
    )
    final = finish(counts, sums, kept, old)
    return place(blocks, stale, final, swap(final))


def solution(mesh):
    mesh = Mesh(mesh.devices.reshape(2, HEAD, SIDE, SIDE), ("branch", "head", "y", "x"))
    seq = ("y", "x")
    in_specs = (
        P("branch", seq, "head"),
        P("branch", None, None),
        P("branch", seq, "head"),
        P("branch", seq, "head"),
        P("branch", seq, "head"),
        P("branch", None, "head"),
        P("branch", "head"),
        P("head", "branch"),
        P("head", "branch"),
        P(),
        P(),
        P(seq, None),
        P(seq),
    )
    out_specs = P(seq, "head")
    return jax.shard_map(local, mesh=mesh, in_specs=in_specs, out_specs=out_specs, check_vma=False)
```

```python
import functools

import jax
import jax.numpy as jnp
from jax import lax
from jax.experimental import pallas as pl
from jax.experimental.pallas import tpu as pltpu
from jax.sharding import Mesh, PartitionSpec as P

HDIM = 128
BLOCK = 128
GUIDANCE = 1.5
EPSILON = 1e-06
LOG2E = 1.4426950408889634
HEAD = 8
SIDE = 4
STALE = 6
STAT_ROWS = 16
MIB = 1024 * 1024

F32 = jnp.float32
BF16 = jnp.bfloat16


def whole():
    return pl.BlockSpec(memory_space=pltpu.VMEM)


def scalars():
    return pl.BlockSpec(memory_space=pltpu.SMEM)


def in_hbm():
    return pl.BlockSpec(memory_space=pltpu.HBM)


def anywhere():
    return pl.BlockSpec(memory_space=pl.ANY)


def params(mebibytes=58):
    return pltpu.CompilerParams(vmem_limit_bytes=mebibytes * MIB)


def dot(left, right):
    return jnp.dot(left, right, preferred_element_type=F32)


def begin(pairs, arrived):
    copies = [
        pltpu.make_async_copy(source, target, arrived.at[i])
        for i, (source, target) in enumerate(pairs)
    ]
    for copy in copies:
        copy.start()
    return copies


def block_rows(number):
    return pl.ds(pl.multiple_of(number * BLOCK, BLOCK), BLOCK)


def pick_kernel(blocks_ref, counts_ref, tokens_ref, k_ref, v_ref, *refs):
    out_ref, packed, stale_s, arrived, sent = refs
    pairs = [
        (tokens_ref.at[block_rows(blocks_ref[0, j])], out_ref.at[pl.ds(j * BLOCK, BLOCK)])
        for j in range(2)
    ]
    low = jnp.minimum(blocks_ref[0, 0], blocks_ref[0, 1])
    high = jnp.maximum(blocks_ref[0, 0], blocks_ref[0, 1])
    for i in range(STALE):
        index = i + (i >= low).astype(jnp.int32)
        index = index + (index >= high).astype(jnp.int32)
        for half, ref in enumerate((k_ref, v_ref)):
            features = pl.ds(2 * half * HDIM, 2 * HDIM)
            pairs.append((ref.at[block_rows(index)], stale_s.at[pl.ds(i * BLOCK, BLOCK), features]))
    copies = begin(pairs, arrived)
    for copy in copies[2:]:
        copy.wait()
    for copy in copies[:2] + begin([(stale_s, packed)], sent):
        copy.wait()


def pick(tokens, keys, values, blocks, counts):
    shape = jax.ShapeDtypeStruct((2 * BLOCK, tokens.shape[1]), BF16)
    stale = jax.ShapeDtypeStruct((STALE * BLOCK, 4 * HDIM), BF16)
    return pl.pallas_call(
        pick_kernel,
        in_specs=[scalars(), scalars()] + [in_hbm()] * 3,
        out_specs=[whole(), in_hbm()],
        out_shape=[shape, stale],
        scratch_shapes=[
            pltpu.VMEM(stale.shape, BF16),
            pltpu.SemaphoreType.DMA((2 + 2 * STALE,)),
            pltpu.SemaphoreType.DMA((1,)),
        ],
        compiler_params=params(),
        name="pick",
    )(blocks, counts, tokens, keys, values)


def project_kernel(blocks_ref, counts_ref, *refs):
    sources = refs[: HEAD + 5]
    keys_ref, values_ref = refs[HEAD + 5 : HEAD + 7]
    fresh_ref, asked_ref, rows_ref = refs[HEAD + 7 : HEAD + 10]
    chunk_s, mod_ref, own_ref, other_ref, q_gain_ref, k_gain_ref, old_s, arrived = refs[HEAD + 10 :]
    core = lax.axis_index("branch")
    z = lax.axis_index("head")
    old = block_rows(blocks_ref[0, 1])
    targets = [chunk_s.at[k] for k in range(HEAD)]
    targets += [mod_ref, own_ref, other_ref, q_gain_ref, k_gain_ref]
    pairs = list(zip(sources, targets))
    pairs += [(keys_ref.at[old], old_s.at[0]), (values_ref.at[old], old_s.at[1])]
    copies = begin(pairs, arrived)
    for copy in copies[: HEAD + 1]:
        copy.wait()
    width = chunk_s.shape[2]
    full = HEAD * width
    step = 32
    for row in range(0, 2 * BLOCK, step):
        values = [chunk_s[k, row : row + step, :].astype(F32) for k in range(HEAD)]
        mean = sum(jnp.sum(v, axis=-1, keepdims=True) for v in values) / full
        centred = [v - mean for v in values]
        var = sum(jnp.sum(c * c, axis=-1, keepdims=True) for c in centred) / full
        inverse = lax.rsqrt(var + EPSILON)
        for k in range(HEAD):
            owner = lax.rem(z - k + HEAD, HEAD)
            columns = pl.ds(pl.multiple_of(owner * width, width), width)
            shift = mod_ref[0, :, columns]
            scale = mod_ref[1, :, columns]
            rows_ref[row : row + step, columns] = (
                centred[k] * inverse * (1.0 + scale) + shift
            ).astype(BF16)
    for copy in copies[HEAD + 1 :]:
        copy.wait()
    half = full // 2
    here = pl.ds(pl.multiple_of(core * half, half), half)
    there = pl.ds(pl.multiple_of((1 - core) * half, half), half)
    query, key, value = (
        dot(rows_ref[:, here], own_ref[i]) + dot(rows_ref[:, there], other_ref[i]) for i in range(3)
    )

    def norm(values, gain_ref):
        power = jnp.mean(values * values, axis=-1, keepdims=True)
        return (values * lax.rsqrt(power + EPSILON) * gain_ref[...]).astype(BF16)

    live = counts_ref[0] > 1
    for head in range(2):
        at = slice(head * HDIM, (head + 1) * HDIM)
        beside = slice((2 + head) * HDIM, (3 + head) * HDIM)
        asked_ref[:, at] = norm(query[:, at], q_gain_ref)
        new_key = norm(key[:, at], k_gain_ref)
        new_value = value[:, at].astype(BF16)
        fresh_ref[:BLOCK, at] = new_key[:BLOCK]
        fresh_ref[:BLOCK, beside] = new_value[:BLOCK]
        fresh_ref[BLOCK:, at] = jnp.where(live, new_key[BLOCK:], old_s[0, :, at])
        fresh_ref[BLOCK:, beside] = jnp.where(live, new_value[BLOCK:], old_s[1, :, at])


def project(blocks, counts, chunks, mod, own, other, q_gain, k_gain, keys, values):
    rows, width = chunks[0].shape
    full = HEAD * width
    sources = [*chunks, mod, own, other, q_gain, k_gain, keys, values]
    return pl.pallas_call(
        project_kernel,
        in_specs=[scalars()] * 2 + [in_hbm()] * len(sources),
        out_specs=[whole()] * 3,
        out_shape=[
            jax.ShapeDtypeStruct((rows, 4 * HDIM), BF16),
            jax.ShapeDtypeStruct((rows, 2 * HDIM), BF16),
            jax.ShapeDtypeStruct((rows, full), BF16),
        ],
        scratch_shapes=[
            pltpu.VMEM((HEAD, rows, width), BF16),
            *[pltpu.VMEM(a.shape, a.dtype) for a in (mod, own, other, q_gain, k_gain)],
            pltpu.VMEM((2, BLOCK, 2 * HDIM), BF16),
            pltpu.SemaphoreType.DMA((len(sources),)),
        ],
        compiler_params=params(),
        cost_estimate=pl.CostEstimate(
            flops=2 * rows * full * 6 * HDIM, bytes_accessed=8 * MIB, transcendentals=0
        ),
        name="project",
    )(blocks, counts, *sources)


def hidden_kernel(rows_ref, own_ref, other_ref, mine_ref, theirs_ref):
    core = lax.axis_index("branch")
    half = own_ref.shape[0]
    here = pl.ds(pl.multiple_of(core * half, half), half)
    there = pl.ds(pl.multiple_of((1 - core) * half, half), half)
    total = dot(rows_ref[:, here], own_ref[...]) + dot(rows_ref[:, there], other_ref[...])
    active = jax.nn.gelu(total, approximate=True).astype(BF16)
    first = core == 0
    mine_ref[...] = jnp.where(first, active[:BLOCK], active[BLOCK:])
    theirs_ref[...] = jnp.where(first, active[BLOCK:], active[:BLOCK])


def hidden_units(rows, own, other):
    units = own.shape[1]
    shape = jax.ShapeDtypeStruct((BLOCK, units), BF16)
    return pl.pallas_call(
        hidden_kernel,
        in_specs=[whole()] * 3,
        out_specs=[whole()] * 2,
        out_shape=[shape, shape],
        compiler_params=params(14),
        cost_estimate=pl.CostEstimate(
            flops=2 * rows.shape[0] * rows.shape[1] * units,
            bytes_accessed=8 * MIB,
            transcendentals=rows.shape[0] * units,
        ),
        name="hidden_units",
    )(rows, own, other)


def gated(mine_ref, theirs_ref, w_own, w_other, mod_own, mod_other, emit):
    core = lax.axis_index("branch")
    factor = jnp.where(core == 0, 1.0 - GUIDANCE, GUIDANCE)
    width = w_own.shape[1] // (HEAD // 2)
    left = jnp.concatenate([mine_ref[...], theirs_ref[...]], axis=0)
    for weights, side in ((w_own, core), (w_other, 1 - core)):
        both = dot(left, weights[...])
        for i in range(HEAD // 2):
            part = both[:, i * width : (i + 1) * width]
            chunk = side * (HEAD // 2) + i
            columns = pl.ds(pl.multiple_of(chunk * width, width), width)
            gate_own = factor * mod_own[2, :, columns]
            gate_other = (1.0 - factor) * mod_other[2, :, columns]
            emit(chunk, part[:BLOCK] * gate_own + part[BLOCK:] * gate_other)


def units_out_kernel(mine_ref, theirs_ref, own_ref, other_ref, mod_ref, mod_other_ref, out_ref):
    def emit(chunk, value):
        out_ref[chunk] = value

    gated(mine_ref, theirs_ref, own_ref, other_ref, mod_ref, mod_other_ref, emit)


def heads_out_kernel(
    mine_ref, theirs_ref, own_ref, other_ref, mod_ref, mod_other_ref, base_ref, out_ref
):
    def emit(chunk, value):
        out_ref[chunk] = (base_ref[chunk] + value).astype(BF16)

    gated(mine_ref, theirs_ref, own_ref, other_ref, mod_ref, mod_other_ref, emit)


def out_product(kernel, dtype, name, limit, mine, theirs, own, other, mod, mod_other, *base):
    width = own.shape[1] // (HEAD // 2)
    return pl.pallas_call(
        kernel,
        in_specs=[whole()] * (6 + len(base)),
        out_specs=whole(),
        out_shape=jax.ShapeDtypeStruct((HEAD, BLOCK, width), dtype),
        compiler_params=params(limit),
        cost_estimate=pl.CostEstimate(
            flops=8 * BLOCK * own.shape[0] * own.shape[1],
            bytes_accessed=6 * MIB,
            transcendentals=0,
        ),
        name=name,
    )(mine, theirs, own, other, mod, mod_other, *base)


def attend_kernel(*refs):
    stale_ref = refs[0]
    fresh, asked = refs[1 : 1 + SIDE], refs[1 + SIDE : 1 + 2 * SIDE]
    outs = refs[-9:-5]
    key_s, score_s, query_s, stat_s, arrived = refs[-5:]
    rows = 2 * BLOCK
    piece = SIDE * rows
    old = stale_ref.shape[0]
    tiles = old // piece + 1
    unit = LOG2E * HDIM**-0.5
    pairs = [(ref, query_s.at[k]) for k, ref in enumerate(asked)]
    pairs += [
        (stale_ref.at[pl.ds(k * piece, piece)], key_s.at[pl.ds(k * piece, piece)])
        for k in range(tiles - 1)
    ]
    pairs += [(fresh[k], key_s.at[pl.ds(old + k * rows, rows)]) for k in range(SIDE)]
    copies = begin(pairs, arrived)
    for copy in copies[:SIDE]:
        copy.wait()
    lane = lax.broadcasted_iota(jnp.int32, (rows, HDIM), 1)
    stat_s[...] = jnp.zeros_like(stat_s)
    for step in range(2 * SIDE):
        head, index = step // SIDE, step % SIDE
        at = slice(head * HDIM, (head + 1) * HDIM)
        beside = slice((2 + head) * HDIM, (3 + head) * HDIM)
        query = query_s[index, :, at]
        top = None
        for k in range(tiles):
            if step == 0:
                for copy in copies[SIDE + k : SIDE + k + 1 if k < tiles - 1 else None]:
                    copy.wait()
            part = key_s[k * piece : (k + 1) * piece, at]
            scores = lax.dot_general(
                query, part, (((1,), (1,)), ((), ())), preferred_element_type=F32
            )
            score_s[:, k * piece : (k + 1) * piece] = scores
            here = jnp.max(scores, axis=-1, keepdims=True)
            top = here if top is None else jnp.maximum(top, here)
        top = top * unit
        total = jnp.zeros((rows, 1), F32)
        summed = jnp.zeros((rows, HDIM), F32)
        for k in range(tiles):
            weights = jnp.exp2(score_s[:, k * piece : (k + 1) * piece] * unit - top)
            total = total + jnp.sum(weights, axis=-1, keepdims=True)
            summed = summed + dot(weights.astype(BF16), key_s[k * piece : (k + 1) * piece, beside])
        outs[index][:rows, at] = (summed / total).astype(BF16)
        stat_s[...] = jnp.where(lane == step, top + jnp.log2(total), stat_s[...])
    stats = jnp.transpose(stat_s[...])
    for step in range(2 * SIDE):
        head, index = step // SIDE, step % SIDE
        row = stats[step : step + 1, :]
        high = row.astype(BF16).astype(F32)
        middle = (row - high).astype(BF16).astype(F32)
        low = row - high - middle
        parts = [p[:, at : at + HDIM] for p in (high, middle, low) for at in (0, HDIM)]
        parts.append(jnp.zeros((STAT_ROWS - 6, HDIM), F32))
        outs[index][rows:, head * HDIM : (head + 1) * HDIM] = jnp.concatenate(
            parts, axis=0
        ).astype(BF16)


def attend(stale, fresh, asked, early):
    rows = 2 * BLOCK
    keys = SIDE * (STALE + 2) * BLOCK
    shape = jax.ShapeDtypeStruct((rows + STAT_ROWS, 2 * HDIM), BF16)
    return pl.pallas_call(
        attend_kernel,
        in_specs=[in_hbm()] * (1 + 2 * SIDE) + [anywhere()] * len(early),
        out_specs=[whole()] * SIDE,
        out_shape=[shape] * SIDE,
        scratch_shapes=[
            pltpu.VMEM((keys, 4 * HDIM), BF16),
            pltpu.VMEM((rows, keys), F32),
            pltpu.VMEM((SIDE, rows, 2 * HDIM), BF16),
            pltpu.VMEM((rows, HDIM), F32),
            pltpu.SemaphoreType.DMA((STALE // 2 + 2 * SIDE,)),
        ],
        compiler_params=params(),
        cost_estimate=pl.CostEstimate(
            flops=8 * SIDE * rows * keys * HDIM,
            bytes_accessed=8 * MIB,
            transcendentals=2 * SIDE * rows * keys,
        ),
        name="attend",
    )(stale, *fresh, *asked, *early)


def join_kernel(*refs):
    parts, (mine_ref, theirs_ref) = refs[:SIDE], refs[SIDE:]
    rows = 2 * BLOCK
    stats = []
    for head in range(2):
        for part in parts:
            tail = part[rows:, head * HDIM : (head + 1) * HDIM].astype(F32)
            joined = [
                jnp.concatenate([tail[i : i + 1], tail[i + 1 : i + 2]], axis=1) for i in (0, 2, 4)
            ]
            stats.append(joined[0] + joined[1] + joined[2])
    stats = jnp.concatenate(stats + [jnp.zeros((HDIM - 2 * SIDE, rows), F32)], axis=0)
    columns = jnp.transpose(stats)
    first = lax.axis_index("branch") == 0
    for head in range(2):
        level = [columns[:, head * SIDE + k : head * SIDE + k + 1] for k in range(SIDE)]
        top = functools.reduce(jnp.maximum, level)
        shares = [jnp.exp2(value - top) for value in level]
        inverse = 1.0 / sum(shares)
        at = slice(head * HDIM, (head + 1) * HDIM)
        result = sum(
            (shares[k] * inverse) * parts[k][:rows, at].astype(F32) for k in range(SIDE)
        ).astype(BF16)
        mine_ref[:, at] = jnp.where(first, result[:BLOCK], result[BLOCK:])
        theirs_ref[:, at] = jnp.where(first, result[BLOCK:], result[:BLOCK])


def join(parts):
    shape = jax.ShapeDtypeStruct((BLOCK, 2 * HDIM), BF16)
    return pl.pallas_call(
        join_kernel,
        in_specs=[whole()] * SIDE,
        out_specs=[whole()] * 2,
        out_shape=[shape, shape],
        compiler_params=params(4),
        name="join",
    )(*parts)


def stale_kernel(
    blocks_ref, mod_ref, mod_other_ref, own_ref, other_ref, cached_ref, cached_other_ref, out_ref,
    kept_ref, old_ref,
):
    core = lax.axis_index("branch")
    factor = jnp.where(core == 0, 1.0 - GUIDANCE, GUIDANCE)
    width = own_ref.shape[1]
    columns = pl.ds(pl.multiple_of(lax.axis_index("head") * width, width), width)
    gate = factor * mod_ref[2, :, columns]
    gate_other = (1.0 - factor) * mod_other_ref[2, :, columns]
    out_ref[...] = (
        factor * own_ref[...].astype(F32)
        + gate * cached_ref[...].astype(F32)
        + (1.0 - factor) * other_ref[...].astype(F32)
        + gate_other * cached_other_ref[...].astype(F32)
    ).astype(BF16)
    rows = block_rows(jnp.where(core == 0, blocks_ref[0, 0], blocks_ref[0, 1]))
    kept_ref[...] = factor * own_ref[rows, :].astype(F32) + (1.0 - factor) * other_ref[
        rows, :
    ].astype(F32)
    old_ref[...] = out_ref[rows, :]


def stale_rows(blocks, mod, mod_other, own, other, cached, cached_other):
    rows, width = own.shape
    return pl.pallas_call(
        stale_kernel,
        in_specs=[scalars()] + [whole()] * 6,
        out_specs=[whole()] * 3,
        out_shape=[
            jax.ShapeDtypeStruct((rows, width), BF16),
            jax.ShapeDtypeStruct((BLOCK, width), F32),
            jax.ShapeDtypeStruct((BLOCK, width), BF16),
        ],
        compiler_params=params(8),
        name="stale_rows",
    )(blocks, mod, mod_other, own, other, cached, cached_other)


def finish_kernel(counts_ref, parts_ref, kept_ref, old_ref, out_ref):
    total = kept_ref[...]
    for k in range(HEAD):
        total = total + parts_ref[k].astype(F32)
    live = lax.axis_index("branch") < counts_ref[0]
    out_ref[...] = jnp.where(live, total.astype(BF16), old_ref[...])


def finish(counts, parts, kept, old):
    return pl.pallas_call(
        finish_kernel,
        in_specs=[scalars()] + [whole()] * 3,
        out_specs=whole(),
        out_shape=jax.ShapeDtypeStruct(old.shape, BF16),
        compiler_params=params(4),
        name="finish",
    )(counts, parts, kept, old)


def place_kernel(blocks_ref, stale_ref, own_ref, other_ref, out_ref, sent):
    core = lax.axis_index("branch")
    copies = []
    for i, ref in enumerate((own_ref, other_ref)):
        first = core == i
        slot = jnp.where(first, blocks_ref[0, 0], blocks_ref[0, 1])
        copies.append(pltpu.make_async_copy(ref, out_ref.at[block_rows(slot)], sent.at[i]))
    for copy in copies:
        copy.start()
    for copy in copies:
        copy.wait()


def place(blocks, stale, own, other):
    return pl.pallas_call(
        place_kernel,
        in_specs=[scalars(), in_hbm(), whole(), whole()],
        out_specs=in_hbm(),
        out_shape=jax.ShapeDtypeStruct(stale.shape, BF16),
        scratch_shapes=[pltpu.SemaphoreType.DMA((2,))],
        input_output_aliases={1: 0},
        compiler_params=params(2),
        name="place",
    )(blocks, stale, own, other)


def ring(array, shift):
    return lax.ppermute(array, "head", [(i, (i + shift) % HEAD) for i in range(HEAD)])


def swap(array):
    return lax.ppermute(array, "branch", [(0, 1), (1, 0)])


def along(axis, array, shift):
    return lax.ppermute(array, axis, [(i, (i + shift) % SIDE) for i in range(SIDE)])


def local(
    hidden,
    modulation,
    branch_cache,
    k_cache,
    v_cache,
    w_qkv,
    w_mlp_in,
    w_attn_out,
    w_mlp_out,
    q_gain,
    k_gain,
    blocks,
    counts,
):
    tokens, cached = hidden[0], branch_cache[0]
    keys, values = k_cache[0], v_cache[0]
    mod = jnp.transpose(modulation, (1, 0, 2))

    picked, stale_here = pick(tokens, keys, values, blocks, counts)
    ups, downs = [picked], [picked]
    for step in range(3):
        ups.append(ring(ups[-1], 1))
        downs.append(ring(downs[-1], -1))
    chunks = ups + [ring(ups[-1], 1)] + downs[:0:-1]

    stale_x = lax.all_gather(stale_here, "x", axis=0, tiled=True)

    qkv = jnp.transpose(w_qkv, (1, 0, 2))
    qkv_other = swap(qkv)
    mod_other = swap(mod)
    mlp_in_other = swap(w_mlp_in)
    mlp_out_other = swap(w_mlp_out)
    attn_out_other = swap(w_attn_out)
    tokens_other = swap(tokens)
    cached_other = swap(cached)

    fresh, asked, rows = project(
        blocks,
        counts,
        chunks,
        mod,
        qkv,
        qkv_other,
        q_gain.reshape(1, HDIM),
        k_gain.reshape(1, HDIM),
        keys,
        values,
    )
    fresh_x = [fresh] + [along("x", fresh, k) for k in range(1, SIDE)]
    asked_y = [asked] + [along("y", asked, k) for k in range(1, SIDE)]

    units, units_send = hidden_units(rows, w_mlp_in, mlp_in_other)
    units_other = swap(units_send)
    base = out_product(
        units_out_kernel, F32, "units_out", 14, units, units_other, w_mlp_out, mlp_out_other,
        mod, mod_other,
    )

    part_y = attend(stale_x, fresh_x, asked_y, [base])
    parts = [part_y[0]] + [along("y", part_y[k], -k) for k in range(1, SIDE)]
    attended, attended_send = join(parts)
    attended_other = swap(attended_send)
    sums = out_product(
        heads_out_kernel, BF16, "heads_out", 10, attended, attended_other, w_attn_out,
        attn_out_other, mod, mod_other, base,
    )
    sums = lax.all_to_all(sums, "head", 0, 0, tiled=True)
    stale, kept, old = stale_rows(
        blocks, mod, mod_other, tokens, tokens_other, cached, cached_other
    )
    final = finish(counts, sums, kept, old)
    return place(blocks, stale, final, swap(final))


def solution(mesh):
    mesh = Mesh(mesh.devices.reshape(2, HEAD, SIDE, SIDE), ("branch", "head", "y", "x"))
    seq = ("y", "x")
    in_specs = (
        P("branch", seq, "head"),
        P("branch", None, None),
        P("branch", seq, "head"),
        P("branch", seq, "head"),
        P("branch", seq, "head"),
        P("branch", None, "head"),
        P("branch", "head"),
        P("head", "branch"),
        P("head", "branch"),
        P(),
        P(),
        P(seq, None),
        P(seq),
    )
    out_specs = P(seq, "head")
    return jax.shard_map(local, mesh=mesh, in_specs=in_specs, out_specs=out_specs, check_vma=False)
```
